32 devices in a mesh: star: 16 (over z, y, x), pix: 2 (over core).
Axes of the slice: x: 2, y: 2, z: 4, core: 2. Of those that a mesh axis runs over, the one named last changes fastest.
Arguments:
- flux: bfloat16 [5120, 8192], P('star', 'pix'), may hold values from -8 to 8
- inv_var: bfloat16 [5120, 8192], P('star', 'pix'), may hold values from 0.099609375 to 10
- coeffs: float32 [231, 8192], P(None, 'pix'), may hold values from -0.375 to 0.375
- labels: float32 [5120, 20], P('star'), may hold values from -4 to 4
Outputs:
- new_coeffs: float32 [231, 8192], P(None, 'pix')
- new_labels: float32 [5120, 20], P('star')
The draws below stay inside these ranges and needn't reach their ends.
All inputs are finite; a program needn't handle non-finite values.
Results may differ from the reference program's by a relative error of at most 0.0087.
Values sent between devices are 32-bit elements; how exact they have to be, the bound alone decides.
No kernel may reach another device: no remote copies, remote signals or barrier semaphores. Data moves between devices by JAX's collectives and lax.ppermute only.
A program may use at most 64 MiB of HBM per device.

```python
import math
import jax
import jax.numpy as jnp
import numpy as np
from jax import lax

PIX = 8192
LABELS = 20
FEAT = 231
ALTS = 2
STARS = 5120


def raised(values, key, source, target, parts, factor):
    owner, partner = [(jnp.arange(values.shape[axis_at]) // (values.shape[axis_at] // parts)).reshape([-1 if axis == axis_at else 1 for axis in range(values.ndim)]) for axis_at in (source, target)]
    chosen = jax.random.permutation(key, parts)[partner]
    strong = (owner == chosen) | (owner == (partner + parts // 2) % parts)
    return jnp.where(strong, factor * values, values)


def block_scale(stream_key, extent, cuts, least, high):
    def one(dim, parts):
        heights = jax.random.uniform(jax.random.fold_in(jax.random.fold_in(stream_key, 6), dim), (parts,), jnp.float32, least / len(cuts), high / len(cuts))
        return jnp.repeat(jnp.exp(heights), extent[dim] // parts).reshape((-1,) + (1,) * (len(extent) - dim - 1))

    factor_of = one(*cuts[0])
    for cut in cuts[1:]:
        factor_of = factor_of * one(*cut)
    return factor_of


def centred(stream_key, extent, deviation, bound, cuts=(), kind=jnp.bfloat16):
    gain = block_scale(stream_key, extent, cuts, -0.22, 0.18) if cuts else 1.0
    result = jax.random.normal(stream_key, extent, jnp.float32) * deviation * gain
    return jnp.minimum(jnp.maximum(result, -bound), bound).astype(kind)


def noise_with(own_key, shape, width, bound, pieces, heavy, kind=jnp.bfloat16):
    entries = width * jax.random.normal(own_key, shape, jnp.float32)
    if pieces:
        entries = entries * block_scale(own_key, shape, pieces, -0.22, 0.18)
    return jnp.clip(raised(entries, jax.random.fold_in(own_key, 3), *heavy), -bound, bound).astype(kind)


def setup_inputs(seed: int = 0) -> dict:
    seeds = jax.random.split(jax.random.key(seed), 5)
    return {
        "flux": noise_with(seeds[0], (STARS, PIX), 1.0, 8.0, ((0, 16), (1, 2)), (0, 1, 16, 2.0)),
        "inv_var": jnp.clip(jnp.exp(math.log(10.0) - 4.609084 * jax.random.uniform(seeds[1], (STARS, PIX), jnp.float32) ** block_scale(seeds[1], (STARS, PIX), ((0, 16), (1, 2)), -0.2, 0.2)), 0.099609375, 10.0).astype(jnp.bfloat16),
        "coeffs": centred(seeds[2], (FEAT, PIX), FEAT ** -0.5, 0.375, ((1, 2),), jnp.float32),
        "labels": centred(seeds[3], (STARS, LABELS), 1.0, 4.0, ((0, 16),), jnp.float32),
    }


step_size = 0.25


def pair_tables(count):
    left_index = []
    right_index = []
    for row_index in range(count):
        for col_index in range(row_index, count):
            left_index.append(row_index)
            right_index.append(col_index)
    pair_table = np.zeros((count, count), np.int32)
    doubling = np.ones((count, count), np.float32)
    for position in range(len(left_index)):
        pair_table[left_index[position], right_index[position]] = 1 + count + position
        pair_table[right_index[position], left_index[position]] = 1 + count + position
    for row_index in range(count):
        doubling[row_index, row_index] = 2.0
    return np.array(left_index, np.int32), np.array(right_index, np.int32), pair_table, doubling


def features(labels):
    left_index, right_index, pair_table, doubling = pair_tables(labels.shape[1])
    quad = labels[:, left_index] * labels[:, right_index]
    ones = jnp.ones((labels.shape[0], 1), labels.dtype)
    return jnp.concatenate([ones, labels, quad], axis=1)


def fdot(left, right):
    return jnp.dot(left.astype(jnp.float32), right.astype(jnp.float32))


def reference(flux, inv_var, coeffs, labels):
    count = labels.shape[1]
    left_index, right_index, pair_table, doubling = pair_tables(count)
    flux_f = flux.astype(jnp.float32)
    ivar_f = inv_var.astype(jnp.float32)
    theta = coeffs
    lab = labels
    for turn in range(ALTS):
        feat = features(lab)
        feat_b = feat.astype(jnp.bfloat16)
        lab_b = lab.astype(jnp.bfloat16)
        sq_b = (feat * feat).astype(jnp.bfloat16)
        theta_b = theta.astype(jnp.bfloat16)
        weighted = (ivar_f * (flux_f - fdot(feat_b, theta_b))).astype(jnp.bfloat16)
        grad = fdot(feat_b.T, weighted)
        curv = 1.0 + fdot(sq_b.T, inv_var)
        theta = theta + step_size * grad / curv
        theta_b = theta.astype(jnp.bfloat16)
        rounded = lax.optimization_barrier((ivar_f * (flux_f - fdot(feat_b, theta_b))).astype(jnp.bfloat16))
        weighted2 = rounded.astype(jnp.float32)
        lead = theta_b[1:1 + count]
        blocks = (theta_b[pair_table.reshape(-1)].astype(jnp.float32) * doubling.reshape(-1, 1)).astype(jnp.bfloat16)
        blocks = blocks.reshape(count, count, theta.shape[1])

        def per_label(item):
            linear, block = item
            jac = linear.astype(jnp.float32)[None, :] + fdot(lab_b, block)
            return jnp.sum(weighted2 * jac, axis=1), jnp.sum(ivar_f * jac * jac, axis=1)

        grads, curvs = lax.map(per_label, (lead, blocks))
        lgrad = grads.T - lab
        lcurv = 1.0 + curvs.T
        lab = lab + lgrad / lcurv
    return theta, lab
```

```python
import functools

import jax
import jax.numpy as jnp
import numpy as np
from jax import lax
from jax.experimental import pallas as pl
from jax.experimental.pallas import tpu as pltpu
from jax.sharding import PartitionSpec as P

ALTS = 2
WAVES = 2
LANES = 128
VMEM_LIMIT = 48 * 1024 * 1024

step_size = 0.25


def pair_tables(count):
    left_index = []
    right_index = []
    for row_index in range(count):
        for col_index in range(row_index, count):
            left_index.append(row_index)
            right_index.append(col_index)
    pair_table = np.zeros((count, count), np.int32)
    doubling = np.ones((count, count), np.float32)
    for position in range(len(left_index)):
        pair_table[left_index[position], right_index[position]] = 1 + count + position
        pair_table[right_index[position], left_index[position]] = 1 + count + position
    for row_index in range(count):
        doubling[row_index, row_index] = 2.0
    return (np.array(left_index, np.int32), np.array(right_index, np.int32), pair_table, doubling)


def round_up(value, unit):
    return -(-value // unit) * unit


def contract_rows(left, right):
    return lax.dot_general(
        left, right, (((0,), (0,)), ((), ())), preferred_element_type=jnp.float32
    )


def plain_device(flux, inv_var, coeffs, labels):
    count = labels.shape[1]
    left_index, right_index, pair_table, doubling = pair_tables(count)
    flux_f = flux.astype(jnp.float32)
    ivar_f = inv_var.astype(jnp.float32)
    theta = coeffs
    lab = labels
    for turn in range(ALTS):
        quad = lab[:, left_index] * lab[:, right_index]
        feat = jnp.concatenate([jnp.ones((lab.shape[0], 1), jnp.float32), lab, quad], axis=1)
        feat_b = feat.astype(jnp.bfloat16)
        lab_b = lab.astype(jnp.bfloat16)
        sq_b = (feat * feat).astype(jnp.bfloat16)
        theta_b = theta.astype(jnp.bfloat16)
        model = jnp.dot(feat_b, theta_b, preferred_element_type=jnp.float32)
        weighted = (ivar_f * (flux_f - model)).astype(jnp.bfloat16)
        grad = contract_rows(feat_b, weighted)
        curv = contract_rows(sq_b, inv_var)
        grad, curv = lax.psum((grad, curv), "star")
        theta = theta + step_size * grad / (1.0 + curv)
        theta_b = theta.astype(jnp.bfloat16)
        model = jnp.dot(feat_b, theta_b, preferred_element_type=jnp.float32)
        rounded = lax.optimization_barrier((ivar_f * (flux_f - model)).astype(jnp.bfloat16))
        weighted2 = rounded.astype(jnp.float32)
        lead = theta_b[1 : 1 + count]
        blocks = (
            theta_b[pair_table.reshape(-1)].astype(jnp.float32) * doubling.reshape(-1, 1)
        ).astype(jnp.bfloat16)
        blocks = blocks.reshape(count, count, theta.shape[1])

        def per_label(item):
            linear, block = item
            jac = linear.astype(jnp.float32)[None, :] + jnp.dot(
                lab_b, block, preferred_element_type=jnp.float32
            )
            return (jnp.sum(weighted2 * jac, axis=1), jnp.sum(ivar_f * jac * jac, axis=1))

        grads, curvs = lax.map(per_label, (lead, blocks))
        lgrad = grads.T
        lcurv = curvs.T
        lgrad, lcurv = lax.psum((lgrad, lcurv), "pix")
        lab = lab + (lgrad - lab) / (1.0 + lcurv)
    return (theta, lab)


def feature_maps(count, padded):
    left_index, right_index, pair_table, doubling = pair_tables(count)
    rows = round_up(1 + count, 32)
    left = np.zeros((rows, padded), np.float32)
    right = np.zeros((rows, padded), np.float32)
    left[0, 0] = 1.0
    right[0, : 1 + count] = 1.0
    for label in range(count):
        left[1 + label, 1 + label] = 1.0
    for position in range(len(left_index)):
        left[1 + left_index[position], 1 + count + position] = 1.0
        right[1 + right_index[position], 1 + count + position] = 1.0
    select = np.zeros((count, rows, padded), np.float32)
    for label in range(count):
        select[label, 0, 1 + label] = 1.0
        for other in range(count):
            select[label, 1 + other, pair_table[label, other]] = doubling[label, other]
    return left, right, select.reshape(count * rows, padded)


def split_exact(value):
    high = value.astype(jnp.bfloat16)
    rest = value - high.astype(jnp.float32)
    middle = rest.astype(jnp.bfloat16)
    low = (rest - middle.astype(jnp.float32)).astype(jnp.bfloat16)
    return high, middle, low


def mm(left, right):
    return jnp.dot(left, right, preferred_element_type=jnp.float32)


def write_features(lab, left_ref, right_ref, feat_ref, featt_ref, sqt_ref, lab1_ref):
    parts = split_exact(lab)
    first = sum(mm(part, left_ref[...]) for part in parts[::-1])
    second = sum(mm(part, right_ref[...]) for part in parts[::-1])
    feat = first * second
    feat_ref[...] = feat.astype(jnp.bfloat16)
    featt_ref[...] = feat.T.astype(jnp.bfloat16)
    sqt_ref[...] = (feat * feat).T.astype(jnp.bfloat16)
    lab1_ref[...] = lab.astype(jnp.bfloat16)


def features_kernel(lab_ref, left_ref, right_ref, *outs):
    write_features(lab_ref[...], left_ref, right_ref, *outs)


def update_kernel(count, lab_ref, here_ref, there_ref, left_ref, right_ref, new_ref, *outs):
    lab = lab_ref[...]
    stars, rows = lab.shape
    total = here_ref[...] + there_ref[...]
    lgrad = total[:, :rows]
    lcurv = total[:, LANES : LANES + rows]
    column = lax.broadcasted_iota(jnp.int32, lab.shape, 1)
    inside = (column >= 1) & (column <= count)
    lab = jnp.where(inside, lab + (lgrad - lab) / (1.0 + lcurv), lab)
    new_ref[...] = lab
    write_features(lab, left_ref, right_ref, *outs)


def theta_pair(refs, spans, first, second):
    columns = []
    for piece in (first, second):
        rows = [ref[piece] for ref in refs]
        columns.append(jnp.concatenate(rows, axis=0))
    return jnp.concatenate(columns, axis=1)


def grad_kernel(plan, from_coeffs, me_ref, *refs):
    n, half, parts = plan["n"], plan["half"], plan["parts"]
    flux_ref, ivar_ref, feat_ref, featt_ref, sqt_ref = refs[:5]
    refs = refs[5:]
    if from_coeffs:
        coeffs_ref, refs = refs[0], refs[1:]
    else:
        thetas, refs = refs[: 2 * len(parts)], refs[2 * len(parts) :]
    sends, keeps = refs[: len(parts)], refs[len(parts) :]
    low = me_ref[0] & (half - 1)
    feat = feat_ref[...]
    for pair in range(half // 2):
        spots = [pl.multiple_of((r ^ low) * LANES, LANES) for r in (2 * pair, 2 * pair + 1)]

        def wide(ref):
            return jnp.concatenate([ref[:, pl.ds(spot, LANES)] for spot in spots], axis=1)

        flux = wide(flux_ref)
        ivar = wide(ivar_ref)
        if from_coeffs:
            theta = wide(coeffs_ref).astype(jnp.bfloat16)
            model = mm(feat[:, : theta.shape[0]], theta)
        else:
            theta = jnp.concatenate(
                [
                    jnp.concatenate(
                        [
                            theta_piece(plan, thetas, part, r)
                            for part in range(len(parts))
                        ],
                        axis=0,
                    )
                    for r in (2 * pair, 2 * pair + 1)
                ],
                axis=1,
            ).astype(jnp.bfloat16)
            model = mm(feat[:, : theta.shape[0]], theta)
        weighted = (ivar.astype(jnp.float32) * (flux.astype(jnp.float32) - model)).astype(jnp.bfloat16)
        grad = mm(featt_ref[...], weighted)
        curv = mm(sqt_ref[...], ivar)
        for side, r in enumerate((2 * pair, 2 * pair + 1)):
            lanes = slice(side * LANES, (side + 1) * LANES)
            for index, part in enumerate(parts):
                upper, spot = place(part["order"], r)
                target = sends[index] if upper else keeps[index]
                rows = slice(part["start"], part["start"] + part["rows"])
                target[spot, 0, 0] = grad[rows, lanes]
                target[spot, 0, 1] = curv[rows, lanes]


def place(order, r):
    bits = [(r >> bit) & 1 for bit in order[:-1]]
    spot = 0
    for bit in bits[1:]:
        spot = 2 * spot + bit
    return bits[0], spot


def theta_piece(plan, thetas, part, r):
    upper, spot = place(plan["parts"][part]["order"], r)
    return thetas[2 * part + upper][spot, 0]


def label_kernel(plan, count, last, me_ref, *refs):
    n, half, parts = plan["n"], plan["half"], plan["parts"]
    flux_ref, ivar_ref, feat_ref, lab1_ref, select_ref = refs[:5]
    thetas = refs[5 : 5 + 2 * len(parts)]
    refs = refs[5 + 2 * len(parts) :]
    sums_ref, refs = refs[0], refs[1:]
    if last:
        new_ref, refs = refs[0], refs[1:]
    dots_ref, squares_ref, iv_ref = refs
    low = me_ref[0] & (half - 1)
    step = pl.program_id(0)
    stars = flux_ref.shape[0]
    rows = lab1_ref.shape[1]

    @pl.when(step == 0)
    def _():
        dots_ref[...] = jnp.zeros_like(dots_ref)
        squares_ref[...] = jnp.zeros_like(squares_ref)

    feat = feat_ref[...]
    for pair in range(half // 2):
        spots = [pl.multiple_of((r ^ low) * LANES, LANES) for r in (2 * pair, 2 * pair + 1)]

        def wide(ref):
            return jnp.concatenate([ref[:, pl.ds(spot, LANES)] for spot in spots], axis=1)

        columns = []
        for r, spot in zip((2 * pair, 2 * pair + 1), spots):
            column = jnp.concatenate(
                [theta_piece(plan, thetas, part, r) for part in range(len(parts))], axis=0
            )
            if last:
                new_ref[:, pl.ds(spot, LANES)] = column[: new_ref.shape[0]]
            columns.append(column)
        theta = jnp.concatenate(columns, axis=1).astype(jnp.bfloat16)
        ivar = wide(ivar_ref).astype(jnp.float32)
        iv_ref[...] = ivar
        model = mm(feat[:, : theta.shape[0]], theta)
        weighted = (ivar * (wide(flux_ref).astype(jnp.float32) - model)).astype(jnp.bfloat16)
        dots_ref[...] += lax.dot_general(
            weighted, theta, (((1,), (1,)), ((), ())), preferred_element_type=jnp.float32
        )
        blocks = mm(select_ref[:, : theta.shape[0]], theta).astype(jnp.bfloat16)
        for label in range(count):
            jac = mm(lab1_ref[...], blocks[label * rows : (label + 1) * rows])
            term = jac * jac * iv_ref[...]
            squares_ref[label] += term[:, :LANES] + term[:, LANES:]

    @pl.when(step == pl.num_programs(0) - 1)
    def _():
        dots = dots_ref[...]
        column = lax.broadcasted_iota(jnp.int32, (stars, LANES), 1)
        lgrad = jnp.zeros((stars, LANES), jnp.float32)
        lcurv = jnp.zeros((stars, LANES), jnp.float32)
        for label in range(count):
            slopes = mm(lab1_ref[...], select_ref[label * rows : (label + 1) * rows, : dots.shape[1]])
            here = column == 1 + label
            lgrad = jnp.where(here, jnp.sum(slopes * dots, axis=1, keepdims=True), lgrad)
            lcurv = jnp.where(here, jnp.sum(squares_ref[label], axis=1, keepdims=True), lcurv)
        sums_ref[:, :LANES] = lgrad
        sums_ref[:, LANES:] = lcurv


def exchange(value, bit, n):
    return lax.ppermute(value, "star", [(d, d ^ (1 << bit)) for d in range(n)])


def pieces_device(plan, flux, inv_var, coeffs, labels):
    n, bits, half, parts = plan["n"], plan["bits"], plan["half"], plan["parts"]
    stars, pixels = flux.shape
    count = labels.shape[1]
    features = coeffs.shape[0]
    padded = plan["padded"]
    height = sum(part["rows"] for part in parts)
    left, right, select = feature_maps(count, padded)
    rows = left.shape[0]
    left = jnp.asarray(left, jnp.bfloat16)
    right = jnp.asarray(right, jnp.bfloat16)
    select = jnp.asarray(select, jnp.bfloat16)
    me = lax.axis_index("star")
    me_vec = me.astype(jnp.int32).reshape(1)
    block = half * LANES
    params = pltpu.CompilerParams(vmem_limit_bytes=VMEM_LIMIT)
    whole = pl.BlockSpec(memory_space=pltpu.VMEM)

    feature_shapes = [
        jax.ShapeDtypeStruct((stars, padded), jnp.bfloat16),
        jax.ShapeDtypeStruct((padded, stars), jnp.bfloat16),
        jax.ShapeDtypeStruct((padded, stars), jnp.bfloat16),
        jax.ShapeDtypeStruct((stars, rows), jnp.bfloat16),
    ]
    lab = jnp.pad(
        jnp.concatenate([jnp.ones((stars, 1), jnp.float32), labels], axis=1),
        ((0, 0), (0, rows - 1 - count)),
    )
    feat, featt, sqt, lab1 = pl.pallas_call(
        features_kernel,
        out_shape=feature_shapes,
        in_specs=[whole] * 3,
        out_specs=[whole] * 4,
        compiler_params=params,
        name="features",
    )(lab, left, right)

    def pixel_spec(height, wave):
        return pl.BlockSpec(
            (height, block), lambda step, me, wave=wave: (0, 2 * wave + (step ^ (me[0] >> (bits - 1))))
        )

    def fixed(array):
        return pl.BlockSpec(array.shape, lambda step, me: (0,) * array.ndim)

    def theta_spec(part):
        return pl.BlockSpec((half // 2, 1, part["rows"], LANES), lambda step, me: (0, step, 0, 0))

    def grad_call(wave, thetas):
        specs = [pixel_spec(stars, wave)] * 2 + [fixed(feat), fixed(featt[:height]), fixed(sqt[:height])]
        operands = [flux, inv_var, feat, featt, sqt]
        if thetas is None:
            specs.append(pixel_spec(features, wave))
            operands.append(coeffs)
        else:
            for part, arrays in zip(parts, thetas):
                specs += [theta_spec(part)] * 2
                operands += list(arrays)
        shapes = [
            jax.ShapeDtypeStruct((half // 2, 2, 2, part["rows"], LANES), jnp.float32) for part in parts
        ] * 2
        out_specs = [
            pl.BlockSpec((half // 2, 1, 2, part["rows"], LANES), lambda step, me: (0, step, 0, 0, 0))
            for part in parts
        ] * 2
        outs = pl.pallas_call(
            functools.partial(grad_kernel, plan, thetas is None),
            out_shape=shapes,
            grid_spec=pltpu.PrefetchScalarGridSpec(
                num_scalar_prefetch=1, grid=(2,), in_specs=specs, out_specs=out_specs
            ),
            compiler_params=params,
            cost_estimate=pl.CostEstimate(
                flops=6 * stars * height * 2 * block,
                bytes_accessed=2 * block * (4 * stars + 12 * height),
                transcendentals=0,
            ),
            name="gradient",
        )(me_vec, *operands)
        flat = [out.reshape((n // 2,) + out.shape[2:]) for out in outs]
        return flat[: len(parts)], flat[len(parts) :]

    def label_call(wave, thetas, last, new):
        specs = [pixel_spec(stars, wave)] * 2 + [fixed(feat), fixed(lab1), fixed(select)]
        operands = [flux, inv_var, feat, lab1, select]
        for part, arrays in zip(parts, thetas):
            specs += [theta_spec(part)] * 2
            operands += list(arrays)
        shapes = [jax.ShapeDtypeStruct((stars, 2 * LANES), jnp.float32)]
        out_specs = [pl.BlockSpec((stars, 2 * LANES), lambda step, me: (0, 0))]
        if last:
            shapes.append(jax.ShapeDtypeStruct((features, 2 * block), jnp.float32))
            out_specs.append(
                pl.BlockSpec((features, block), lambda step, me: (0, step ^ (me[0] >> (bits - 1))))
            )
        outs = pl.pallas_call(
            functools.partial(label_kernel, plan, count, last),
            out_shape=shapes,
            grid_spec=pltpu.PrefetchScalarGridSpec(
                num_scalar_prefetch=1,
                grid=(2,),
                in_specs=specs,
                out_specs=out_specs,
                scratch_shapes=[
                    pltpu.VMEM((stars, height), jnp.float32),
                    pltpu.VMEM((count, stars, LANES), jnp.float32),
                    pltpu.VMEM((stars, 2 * LANES), jnp.float32),
                ],
            ),
            compiler_params=params,
            cost_estimate=pl.CostEstimate(
                flops=2 * stars * 256 * 2 * block * (count + 2),
                bytes_accessed=2 * block * (4 * stars + 4 * height),
                transcendentals=0,
            ),
            name="labels",
        )(me_vec, *operands)
        return outs

    base = jnp.pad(
        jnp.stack(
            [
                lax.dynamic_slice(coeffs, (0, (wave * n + me) * LANES), (features, LANES))
                for wave in range(WAVES)
            ]
        ),
        ((0, 0), (0, height - features), (0, 0)),
    )
    own = [
        [base[wave, part["start"] : part["start"] + part["rows"]] for part in parts]
        for wave in range(WAVES)
    ]
    thetas = [None] * WAVES
    for turn in range(ALTS):
        last = turn == ALTS - 1
        sums = None
        news = []
        for wave in range(WAVES):
            sends, keeps = grad_call(wave, thetas[wave])
            gathered = []
            for index, part in enumerate(parts):
                order = part["order"]
                kept = [keeps[index]]
                arrived = exchange(sends[index], order[0], n)
                size = n // 2
                for bit in order[1:]:
                    kept.append(arrived)
                    size //= 2
                    outgoing = sum(array[size : 2 * size] for array in kept)
                    arrived = exchange(outgoing, bit, n)
                kept.append(arrived)
                total = sum(array[0] for array in kept)
                own[wave][index] = own[wave][index] + step_size * total[0] / (1.0 + total[1])
                held = own[wave][index][None]
                for bit in order[:0:-1]:
                    held = jnp.concatenate([held, exchange(held, bit, n)], axis=0)
                other = exchange(held, order[0], n)
                gathered.append(
                    [array.reshape((n // 4, 2) + array.shape[1:]) for array in (held, other)]
                )
            thetas[wave] = gathered
        for wave in range(WAVES):
            outs = label_call(wave, thetas[wave], last, None)
            sums = outs[0] if sums is None else sums + outs[0]
            if last:
                news.append(outs[1])
        there = lax.ppermute(sums, "pix", plan["swap"])
        new_lab, feat, featt, sqt, lab1 = pl.pallas_call(
            functools.partial(update_kernel, count),
            out_shape=[jax.ShapeDtypeStruct((stars, rows), jnp.float32)] + feature_shapes,
            in_specs=[whole] * 5,
            out_specs=[whole] * 5,
            compiler_params=params,
            name="update",
        )(lab, sums, there, left, right)
        lab = new_lab
    return jnp.concatenate(news, axis=1), lab[:, 1 : 1 + count]


def make_plan(mesh, flux, coeffs):
    n = mesh.shape["star"]
    bits = n.bit_length() - 1
    stars = flux.shape[0] // n
    pixels = flux.shape[1] // mesh.shape["pix"]
    if n != 1 << bits or bits < 4 or mesh.shape["pix"] != 2:
        return None
    if pixels != WAVES * n * LANES or stars % 16:
        return None
    height = round_up(coeffs.shape[0], 8)
    first = round_up(int(0.4 * height), 16)
    second = round_up(int(0.34 * height), 16)
    cuts = [0, first, first + second, height]
    rest = list(range(3, bits))
    orders = [[0, 1, 2] + rest, [1, 2, 0] + rest, [2, 0, 1] + rest]
    parts = [
        {"start": cuts[i], "rows": cuts[i + 1] - cuts[i], "order": orders[i]} for i in range(3)
    ]
    return {
        "n": n,
        "bits": bits,
        "half": n // 2,
        "parts": parts,
        "padded": round_up(coeffs.shape[0], 256),
        "swap": [(0, 1), (1, 0)],
    }


def solution(mesh):
    in_specs = (P("star", "pix"), P("star", "pix"), P(None, "pix"), P("star", None))
    out_specs = (P(None, "pix"), P("star", None))

    def run(flux, inv_var, coeffs, labels):
        plan = make_plan(mesh, flux, coeffs)
        body = plain_device if plan is None else functools.partial(pieces_device, plan)
        return jax.shard_map(
            body, mesh=mesh, in_specs=in_specs, out_specs=out_specs, check_vma=False
        )(flux, inv_var, coeffs, labels)

    return run
```

```python
import functools

import jax
import jax.numpy as jnp
import numpy as np
from jax import lax
from jax.experimental import pallas as pl
from jax.experimental.pallas import tpu as pltpu
from jax.sharding import PartitionSpec as P

ALTS = 2
WAVES = 1
LANES = 128
VMEM_LIMIT = 48 * 1024 * 1024

step_size = 0.25


def pair_tables(count):
    left_index = []
    right_index = []
    for row_index in range(count):
        for col_index in range(row_index, count):
            left_index.append(row_index)
            right_index.append(col_index)
    pair_table = np.zeros((count, count), np.int32)
    doubling = np.ones((count, count), np.float32)
    for position in range(len(left_index)):
        pair_table[left_index[position], right_index[position]] = 1 + count + position
        pair_table[right_index[position], left_index[position]] = 1 + count + position
    for row_index in range(count):
        doubling[row_index, row_index] = 2.0
    return (np.array(left_index, np.int32), np.array(right_index, np.int32), pair_table, doubling)


def round_up(value, unit):
    return -(-value // unit) * unit


def contract_rows(left, right):
    return lax.dot_general(
        left, right, (((0,), (0,)), ((), ())), preferred_element_type=jnp.float32
    )


def plain_device(flux, inv_var, coeffs, labels):
    count = labels.shape[1]
    left_index, right_index, pair_table, doubling = pair_tables(count)
    flux_f = flux.astype(jnp.float32)
    ivar_f = inv_var.astype(jnp.float32)
    theta = coeffs
    lab = labels
    for turn in range(ALTS):
        quad = lab[:, left_index] * lab[:, right_index]
        feat = jnp.concatenate([jnp.ones((lab.shape[0], 1), jnp.float32), lab, quad], axis=1)
        feat_b = feat.astype(jnp.bfloat16)
        lab_b = lab.astype(jnp.bfloat16)
        sq_b = (feat * feat).astype(jnp.bfloat16)
        theta_b = theta.astype(jnp.bfloat16)
        model = jnp.dot(feat_b, theta_b, preferred_element_type=jnp.float32)
        weighted = (ivar_f * (flux_f - model)).astype(jnp.bfloat16)
        grad = contract_rows(feat_b, weighted)
        curv = contract_rows(sq_b, inv_var)
        grad, curv = lax.psum((grad, curv), "star")
        theta = theta + step_size * grad / (1.0 + curv)
        theta_b = theta.astype(jnp.bfloat16)
        model = jnp.dot(feat_b, theta_b, preferred_element_type=jnp.float32)
        rounded = lax.optimization_barrier((ivar_f * (flux_f - model)).astype(jnp.bfloat16))
        weighted2 = rounded.astype(jnp.float32)
        lead = theta_b[1 : 1 + count]
        blocks = (
            theta_b[pair_table.reshape(-1)].astype(jnp.float32) * doubling.reshape(-1, 1)
        ).astype(jnp.bfloat16)
        blocks = blocks.reshape(count, count, theta.shape[1])

        def per_label(item):
            linear, block = item
            jac = linear.astype(jnp.float32)[None, :] + jnp.dot(
                lab_b, block, preferred_element_type=jnp.float32
            )
            return (jnp.sum(weighted2 * jac, axis=1), jnp.sum(ivar_f * jac * jac, axis=1))

        grads, curvs = lax.map(per_label, (lead, blocks))
        lgrad = grads.T
        lcurv = curvs.T
        lgrad, lcurv = lax.psum((lgrad, lcurv), "pix")
        lab = lab + (lgrad - lab) / (1.0 + lcurv)
    return (theta, lab)


def feature_maps(count, padded):
    left_index, right_index, pair_table, doubling = pair_tables(count)
    rows = round_up(1 + count, 32)
    left = np.zeros((rows, padded), np.float32)
    right = np.zeros((rows, padded), np.float32)
    left[0, 0] = 1.0
    right[0, : 1 + count] = 1.0
    for label in range(count):
        left[1 + label, 1 + label] = 1.0
    for position in range(len(left_index)):
        left[1 + left_index[position], 1 + count + position] = 1.0
        right[1 + right_index[position], 1 + count + position] = 1.0
    select = np.zeros((count, rows, padded), np.float32)
    for label in range(count):
        select[label, 0, 1 + label] = 1.0
        for other in range(count):
            select[label, 1 + other, pair_table[label, other]] = doubling[label, other]
    return left, right, select.reshape(count * rows, padded)


def split_exact(value):
    high = value.astype(jnp.bfloat16)
    rest = value - high.astype(jnp.float32)
    middle = rest.astype(jnp.bfloat16)
    low = (rest - middle.astype(jnp.float32)).astype(jnp.bfloat16)
    return high, middle, low


def mm(left, right):
    return jnp.dot(left, right, preferred_element_type=jnp.float32)


def write_features(lab, left_ref, right_ref, feat_ref, featt_ref, sqt_ref, lab1_ref):
    parts = split_exact(lab)
    first = sum(mm(part, left_ref[...]) for part in parts[::-1])
    second = sum(mm(part, right_ref[...]) for part in parts[::-1])
    feat = first * second
    feat_ref[...] = feat.astype(jnp.bfloat16)
    featt_ref[...] = feat.T.astype(jnp.bfloat16)
    sqt_ref[...] = (feat * feat).T.astype(jnp.bfloat16)
    lab1_ref[...] = lab.astype(jnp.bfloat16)


def features_kernel(lab_ref, left_ref, right_ref, *outs):
    write_features(lab_ref[...], left_ref, right_ref, *outs)


def update_kernel(count, lab_ref, here_ref, there_ref, left_ref, right_ref, new_ref, *outs):
    lab = lab_ref[...]
    stars, rows = lab.shape
    total = here_ref[...] + there_ref[...]
    lgrad = total[:, :rows]
    lcurv = total[:, LANES : LANES + rows]
    column = lax.broadcasted_iota(jnp.int32, lab.shape, 1)
    inside = (column >= 1) & (column <= count)
    lab = jnp.where(inside, lab + (lgrad - lab) / (1.0 + lcurv), lab)
    new_ref[...] = lab
    write_features(lab, left_ref, right_ref, *outs)


def grad_kernel(plan, from_coeffs, me_ref, *refs):
    n, half, parts = plan["n"], plan["half"], plan["parts"]
    flux_ref, ivar_ref, feat_ref, featt_ref, sqt_ref = refs[:5]
    refs = refs[5:]
    if from_coeffs:
        coeffs_ref, refs = refs[0], refs[1:]
    else:
        thetas, refs = refs[: 2 * len(parts)], refs[2 * len(parts) :]
    sends, keeps = refs[: len(parts)], refs[len(parts) :]
    low = me_ref[0] & (half - 1)
    feat = feat_ref[...]
    width = plan["lanes"]
    for r in range(half):
        lanes = pl.ds(pl.multiple_of((r ^ low) * width, width), width)
        flux = flux_ref[:, lanes]
        ivar = ivar_ref[:, lanes]
        if from_coeffs:
            theta = coeffs_ref[:, lanes].astype(jnp.bfloat16)
        else:
            theta = theta_piece(plan, thetas, r).astype(jnp.bfloat16)
        model = mm(feat[:, : theta.shape[0]], theta)
        weighted = (ivar.astype(jnp.float32) * (flux.astype(jnp.float32) - model)).astype(jnp.bfloat16)
        grad = mm(featt_ref[...], weighted)
        curv = mm(sqt_ref[...], ivar)
        for index, part in enumerate(parts):
            upper, spot = place(part["order"], r)
            target = sends[index] if upper else keeps[index]
            rows = slice(part["start"], part["start"] + part["rows"])
            target[spot, 0, 0] = grad[rows]
            target[spot, 0, 1] = curv[rows]


def place(order, r):
    bits = [(r >> bit) & 1 for bit in order[:-1]]
    spot = 0
    for bit in bits[1:]:
        spot = 2 * spot + bit
    return bits[0], spot


def theta_piece(plan, thetas, r):
    rows = []
    for index, part in enumerate(plan["parts"]):
        upper, spot = place(part["order"], r)
        rows.append(thetas[2 * index + upper][spot, 0])
    return jnp.concatenate(rows, axis=0)


def label_kernel(plan, count, last, me_ref, *refs):
    n, half, parts = plan["n"], plan["half"], plan["parts"]
    flux_ref, ivar_ref, feat_ref, lab1_ref, select_ref = refs[:5]
    thetas = refs[5 : 5 + 2 * len(parts)]
    refs = refs[5 + 2 * len(parts) :]
    sums_ref, refs = refs[0], refs[1:]
    if last:
        new_ref, refs = refs[0], refs[1:]
    dots_ref, squares_ref, iv_ref = refs
    low = me_ref[0] & (half - 1)
    step = pl.program_id(0)
    stars = flux_ref.shape[0]
    rows = lab1_ref.shape[1]

    @pl.when(step == 0)
    def _():
        dots_ref[...] = jnp.zeros_like(dots_ref)
        squares_ref[...] = jnp.zeros_like(squares_ref)

    feat = feat_ref[...]
    width = plan["lanes"]
    for r in range(half):
        lanes = pl.ds(pl.multiple_of((r ^ low) * width, width), width)
        column = theta_piece(plan, thetas, r)
        if last:
            new_ref[:, lanes] = column[: new_ref.shape[0]]
        theta = column.astype(jnp.bfloat16)
        ivar = ivar_ref[:, lanes].astype(jnp.float32)
        iv_ref[...] = ivar
        model = mm(feat[:, : theta.shape[0]], theta)
        weighted = (ivar * (flux_ref[:, lanes].astype(jnp.float32) - model)).astype(jnp.bfloat16)
        dots_ref[...] += lax.dot_general(
            weighted, theta, (((1,), (1,)), ((), ())), preferred_element_type=jnp.float32
        )
        blocks = mm(select_ref[:, : theta.shape[0]], theta).astype(jnp.bfloat16)
        for label in range(count):
            jac = mm(lab1_ref[...], blocks[label * rows : (label + 1) * rows])
            term = jac * jac * iv_ref[...]
            squares_ref[label] += sum(term[:, at : at + LANES] for at in range(0, width, LANES))

    @pl.when(step == pl.num_programs(0) - 1)
    def _():
        dots = dots_ref[...]
        column = lax.broadcasted_iota(jnp.int32, (stars, LANES), 1)
        lgrad = jnp.zeros((stars, LANES), jnp.float32)
        lcurv = jnp.zeros((stars, LANES), jnp.float32)
        for label in range(count):
            slopes = mm(lab1_ref[...], select_ref[label * rows : (label + 1) * rows, : dots.shape[1]])
            here = column == 1 + label
            lgrad = jnp.where(here, jnp.sum(slopes * dots, axis=1, keepdims=True), lgrad)
            lcurv = jnp.where(here, jnp.sum(squares_ref[label], axis=1, keepdims=True), lcurv)
        sums_ref[:, :LANES] = lgrad
        sums_ref[:, LANES:] = lcurv


def exchange(value, bit, n):
    return lax.ppermute(value, "star", [(d, d ^ (1 << bit)) for d in range(n)])


def pieces_device(plan, flux, inv_var, coeffs, labels):
    n, bits, half, parts = plan["n"], plan["bits"], plan["half"], plan["parts"]
    stars, pixels = flux.shape
    count = labels.shape[1]
    features = coeffs.shape[0]
    padded = plan["padded"]
    height = sum(part["rows"] for part in parts)
    left, right, select = feature_maps(count, padded)
    rows = left.shape[0]
    left = jnp.asarray(left, jnp.bfloat16)
    right = jnp.asarray(right, jnp.bfloat16)
    select = jnp.asarray(select, jnp.bfloat16)
    me = lax.axis_index("star")
    me_vec = me.astype(jnp.int32).reshape(1)
    width = plan["lanes"]
    block = half * width
    params = pltpu.CompilerParams(vmem_limit_bytes=VMEM_LIMIT)
    whole = pl.BlockSpec(memory_space=pltpu.VMEM)

    feature_shapes = [
        jax.ShapeDtypeStruct((stars, padded), jnp.bfloat16),
        jax.ShapeDtypeStruct((padded, stars), jnp.bfloat16),
        jax.ShapeDtypeStruct((padded, stars), jnp.bfloat16),
        jax.ShapeDtypeStruct((stars, rows), jnp.bfloat16),
    ]
    lab = jnp.pad(
        jnp.concatenate([jnp.ones((stars, 1), jnp.float32), labels], axis=1),
        ((0, 0), (0, rows - 1 - count)),
    )
    feat, featt, sqt, lab1 = pl.pallas_call(
        features_kernel,
        out_shape=feature_shapes,
        in_specs=[whole] * 3,
        out_specs=[whole] * 4,
        compiler_params=params,
        name="features",
    )(lab, left, right)

    def pixel_spec(height, wave):
        return pl.BlockSpec(
            (height, block), lambda step, me, wave=wave: (0, 2 * wave + (step ^ (me[0] >> (bits - 1))))
        )

    def fixed(array):
        return pl.BlockSpec(array.shape, lambda step, me: (0,) * array.ndim)

    def theta_spec(part):
        return pl.BlockSpec((half // 2, 1, part["rows"], width), lambda step, me: (0, step, 0, 0))

    def grad_call(wave, thetas):
        specs = [pixel_spec(stars, wave)] * 2 + [fixed(feat), fixed(featt), fixed(sqt)]
        operands = [flux, inv_var, feat, featt, sqt]
        if thetas is None:
            specs.append(pixel_spec(features, wave))
            operands.append(coeffs)
        else:
            for part, arrays in zip(parts, thetas):
                specs += [theta_spec(part)] * 2
                operands += list(arrays)
        shapes = [
            jax.ShapeDtypeStruct((half // 2, 2, 2, part["rows"], width), jnp.float32) for part in parts
        ] * 2
        out_specs = [
            pl.BlockSpec((half // 2, 1, 2, part["rows"], width), lambda step, me: (0, step, 0, 0, 0))
            for part in parts
        ] * 2
        outs = pl.pallas_call(
            functools.partial(grad_kernel, plan, thetas is None),
            out_shape=shapes,
            grid_spec=pltpu.PrefetchScalarGridSpec(
                num_scalar_prefetch=1, grid=(2,), in_specs=specs, out_specs=out_specs
            ),
            compiler_params=params,
            cost_estimate=pl.CostEstimate(
                flops=6 * stars * height * 2 * block,
                bytes_accessed=2 * block * (4 * stars + 12 * height),
                transcendentals=0,
            ),
            name="gradient",
        )(me_vec, *operands)
        flat = [out.reshape((n // 2,) + out.shape[2:]) for out in outs]
        return flat[: len(parts)], flat[len(parts) :]

    def label_call(wave, thetas, last, new):
        specs = [pixel_spec(stars, wave)] * 2 + [fixed(feat), fixed(lab1), fixed(select)]
        operands = [flux, inv_var, feat, lab1, select]
        for part, arrays in zip(parts, thetas):
            specs += [theta_spec(part)] * 2
            operands += list(arrays)
        shapes = [jax.ShapeDtypeStruct((stars, 2 * LANES), jnp.float32)]
        out_specs = [pl.BlockSpec((stars, 2 * LANES), lambda step, me: (0, 0))]
        if last:
            shapes.append(jax.ShapeDtypeStruct((features, 2 * block), jnp.float32))
            out_specs.append(
                pl.BlockSpec((features, block), lambda step, me: (0, step ^ (me[0] >> (bits - 1))))
            )
        outs = pl.pallas_call(
            functools.partial(label_kernel, plan, count, last),
            out_shape=shapes,
            grid_spec=pltpu.PrefetchScalarGridSpec(
                num_scalar_prefetch=1,
                grid=(2,),
                in_specs=specs,
                out_specs=out_specs,
                scratch_shapes=[
                    pltpu.VMEM((stars, height), jnp.float32),
                    pltpu.VMEM((count, stars, LANES), jnp.float32),
                    pltpu.VMEM((stars, width), jnp.float32),
                ],
            ),
            compiler_params=params,
            cost_estimate=pl.CostEstimate(
                flops=2 * stars * 256 * 2 * block * (count + 2),
                bytes_accessed=2 * block * (4 * stars + 4 * height),
                transcendentals=0,
            ),
            name="labels",
        )(me_vec, *operands)
        return outs

    base = jnp.pad(
        jnp.stack(
            [
                lax.dynamic_slice(coeffs, (0, (wave * n + me) * width), (features, width))
                for wave in range(WAVES)
            ]
        ),
        ((0, 0), (0, height - features), (0, 0)),
    )
    own = [
        [base[wave, part["start"] : part["start"] + part["rows"]] for part in parts]
        for wave in range(WAVES)
    ]
    thetas = [None] * WAVES
    for turn in range(ALTS):
        last = turn == ALTS - 1
        sums = None
        news = []
        for wave in range(WAVES):
            sends, keeps = grad_call(wave, thetas[wave])
            gathered = []
            for index, part in enumerate(parts):
                order = part["order"]
                kept = [keeps[index]]
                arrived = exchange(sends[index], order[0], n)
                size = n // 2
                for bit in order[1:]:
                    kept.append(arrived)
                    size //= 2
                    outgoing = sum(array[size : 2 * size] for array in kept)
                    arrived = exchange(outgoing, bit, n)
                kept.append(arrived)
                total = sum(array[0] for array in kept)
                own[wave][index] = own[wave][index] + step_size * total[0] / (1.0 + total[1])
                held = own[wave][index][None]
                for bit in order[:0:-1]:
                    held = jnp.concatenate([held, exchange(held, bit, n)], axis=0)
                other = exchange(held, order[0], n)
                gathered.append(
                    [array.reshape((n // 4, 2) + array.shape[1:]) for array in (held, other)]
                )
            thetas[wave] = gathered
        for wave in range(WAVES):
            outs = label_call(wave, thetas[wave], last, None)
            sums = outs[0] if sums is None else sums + outs[0]
            if last:
                news.append(outs[1])
        there = lax.ppermute(sums, "pix", plan["swap"])
        new_lab, feat, featt, sqt, lab1 = pl.pallas_call(
            functools.partial(update_kernel, count),
            out_shape=[jax.ShapeDtypeStruct((stars, rows), jnp.float32)] + feature_shapes,
            in_specs=[whole] * 5,
            out_specs=[whole] * 5,
            compiler_params=params,
            name="update",
        )(lab, sums, there, left, right)
        lab = new_lab
    return jnp.concatenate(news, axis=1) if WAVES > 1 else news[0], lab[:, 1 : 1 + count]


def make_plan(mesh, flux, coeffs):
    n = mesh.shape["star"]
    bits = n.bit_length() - 1
    stars = flux.shape[0] // n
    pixels = flux.shape[1] // mesh.shape["pix"]
    if n != 1 << bits or bits < 4 or mesh.shape["pix"] != 2:
        return None
    if pixels % (WAVES * n * LANES) or stars % 16:
        return None
    height = round_up(coeffs.shape[0], 8)
    first = second = round_up(height // 3, 16)
    cuts = [0, first, first + second, height]
    rest = list(range(3, bits))
    orders = [[0, 1, 2] + rest, [1, 2, 0] + rest, [2, 0, 1] + rest]
    parts = [
        {"start": cuts[i], "rows": cuts[i + 1] - cuts[i], "order": orders[i]} for i in range(3)
    ]
    return {
        "n": n,
        "bits": bits,
        "half": n // 2,
        "lanes": pixels // (WAVES * n),
        "parts": parts,
        "padded": round_up(coeffs.shape[0], 256),
        "swap": [(0, 1), (1, 0)],
    }


def solution(mesh):
    in_specs = (P("star", "pix"), P("star", "pix"), P(None, "pix"), P("star", None))
    out_specs = (P(None, "pix"), P("star", None))

    def run(flux, inv_var, coeffs, labels):
        plan = make_plan(mesh, flux, coeffs)
        body = plain_device if plan is None else functools.partial(pieces_device, plan)
        return jax.shard_map(
            body, mesh=mesh, in_specs=in_specs, out_specs=out_specs, check_vma=False
        )(flux, inv_var, coeffs, labels)

    return run
```

```python
import functools

import jax
import jax.numpy as jnp
import numpy as np
from jax import lax
from jax.experimental import pallas as pl
from jax.experimental.pallas import tpu as pltpu
from jax.sharding import PartitionSpec as P

ALTS = 2
LANES = 128
VMEM_LIMIT = 16 * 1024 * 1024

step_size = 0.25


def pair_tables(count):
    left_index = []
    right_index = []
    for row_index in range(count):
        for col_index in range(row_index, count):
            left_index.append(row_index)
            right_index.append(col_index)
    pair_table = np.zeros((count, count), np.int32)
    doubling = np.ones((count, count), np.float32)
    for position in range(len(left_index)):
        pair_table[left_index[position], right_index[position]] = 1 + count + position
        pair_table[right_index[position], left_index[position]] = 1 + count + position
    for row_index in range(count):
        doubling[row_index, row_index] = 2.0
    return (np.array(left_index, np.int32), np.array(right_index, np.int32), pair_table, doubling)


def round_up(value, unit):
    return -(-value // unit) * unit


def contract_rows(left, right):
    return lax.dot_general(
        left, right, (((0,), (0,)), ((), ())), preferred_element_type=jnp.float32
    )


def plain_device(flux, inv_var, coeffs, labels):
    count = labels.shape[1]
    left_index, right_index, pair_table, doubling = pair_tables(count)
    flux_f = flux.astype(jnp.float32)
    ivar_f = inv_var.astype(jnp.float32)
    theta = coeffs
    lab = labels
    for turn in range(ALTS):
        quad = lab[:, left_index] * lab[:, right_index]
        feat = jnp.concatenate([jnp.ones((lab.shape[0], 1), jnp.float32), lab, quad], axis=1)
        feat_b = feat.astype(jnp.bfloat16)
        lab_b = lab.astype(jnp.bfloat16)
        sq_b = (feat * feat).astype(jnp.bfloat16)
        theta_b = theta.astype(jnp.bfloat16)
        model = jnp.dot(feat_b, theta_b, preferred_element_type=jnp.float32)
        weighted = (ivar_f * (flux_f - model)).astype(jnp.bfloat16)
        grad = contract_rows(feat_b, weighted)
        curv = contract_rows(sq_b, inv_var)
        grad, curv = lax.psum((grad, curv), "star")
        theta = theta + step_size * grad / (1.0 + curv)
        theta_b = theta.astype(jnp.bfloat16)
        model = jnp.dot(feat_b, theta_b, preferred_element_type=jnp.float32)
        rounded = lax.optimization_barrier((ivar_f * (flux_f - model)).astype(jnp.bfloat16))
        weighted2 = rounded.astype(jnp.float32)
        lead = theta_b[1 : 1 + count]
        blocks = (
            theta_b[pair_table.reshape(-1)].astype(jnp.float32) * doubling.reshape(-1, 1)
        ).astype(jnp.bfloat16)
        blocks = blocks.reshape(count, count, theta.shape[1])

        def per_label(item):
            linear, block = item
            jac = linear.astype(jnp.float32)[None, :] + jnp.dot(
                lab_b, block, preferred_element_type=jnp.float32
            )
            return (jnp.sum(weighted2 * jac, axis=1), jnp.sum(ivar_f * jac * jac, axis=1))

        grads, curvs = lax.map(per_label, (lead, blocks))
        lgrad = grads.T
        lcurv = curvs.T
        lgrad, lcurv = lax.psum((lgrad, lcurv), "pix")
        lab = lab + (lgrad - lab) / (1.0 + lcurv)
    return (theta, lab)


def feature_maps(count, padded):
    left_index, right_index, pair_table, doubling = pair_tables(count)
    rows = round_up(1 + count, 32)
    left = np.zeros((rows, padded), np.float32)
    right = np.zeros((rows, padded), np.float32)
    left[0, 0] = 1.0
    right[0, : 1 + count] = 1.0
    for label in range(count):
        left[1 + label, 1 + label] = 1.0
    for position in range(len(left_index)):
        left[1 + left_index[position], 1 + count + position] = 1.0
        right[1 + right_index[position], 1 + count + position] = 1.0
    select = np.zeros((count, rows, padded), np.float32)
    for label in range(count):
        select[label, 0, 1 + label] = 1.0
        for other in range(count):
            select[label, 1 + other, pair_table[label, other]] = doubling[label, other]
    return left, right, select.reshape(count * rows, padded)


def split_exact(value):
    high = value.astype(jnp.bfloat16)
    rest = value - high.astype(jnp.float32)
    middle = rest.astype(jnp.bfloat16)
    low = (rest - middle.astype(jnp.float32)).astype(jnp.bfloat16)
    return high, middle, low


def mm(left, right):
    return jnp.dot(left, right, preferred_element_type=jnp.float32)


def write_features(lab, left_ref, right_ref, feat_ref, featt_ref, sqt_ref, lab1_ref):
    parts = split_exact(lab)
    first = sum(mm(part, left_ref[...]) for part in parts[::-1])
    second = sum(mm(part, right_ref[...]) for part in parts[::-1])
    feat = first * second
    feat_ref[...] = feat.astype(jnp.bfloat16)
    featt_ref[...] = feat.T.astype(jnp.bfloat16)
    sqt_ref[...] = (feat * feat).T.astype(jnp.bfloat16)
    lab1_ref[...] = lab.astype(jnp.bfloat16)


def features_kernel(lab_ref, left_ref, right_ref, *outs):
    write_features(lab_ref[...], left_ref, right_ref, *outs)


def update_kernel(count, lab_ref, here_ref, there_ref, left_ref, right_ref, new_ref, *outs):
    lab = lab_ref[...]
    stars, rows = lab.shape
    total = here_ref[...] + there_ref[...]
    lgrad = total[:, :rows]
    lcurv = total[:, LANES : LANES + rows]
    column = lax.broadcasted_iota(jnp.int32, lab.shape, 1)
    inside = (column >= 1) & (column <= count)
    lab = jnp.where(inside, lab + (lgrad - lab) / (1.0 + lcurv), lab)
    new_ref[...] = lab
    write_features(lab, left_ref, right_ref, *outs)


def place(order, r):
    bits = [(r >> bit) & 1 for bit in order]
    spot = 0
    for bit in bits[1:]:
        spot = 2 * spot + bit
    return bits[0], spot


def load_chains(chains, refs, r):
    rows = []
    for index, chain in enumerate(chains):
        upper, spot = place(chain["order"], r)
        rows.append(refs[2 * index + upper][spot])
    return jnp.concatenate(rows, axis=0)


def swapped(bits):
    return (bits & ~12) | ((bits & 4) << 1) | ((bits >> 1) & 4)


def lanes_of(me_ref, r, width):
    piece = (r + me_ref[1] * (swapped(r) - r)) ^ me_ref[0]
    return pl.ds(pl.multiple_of(piece * width, width), width)


def gradient_kernel(plan, from_coeffs, me_ref, flux_ref, ivar_ref, feat_ref, featt_ref, sqt_ref, *refs):
    height = plan["height"]
    if from_coeffs:
        coeffs_ref, outs = refs[0], refs[1:]
    else:
        thetas, outs = refs[: 2 * len(plan["parts"])], refs[2 * len(plan["parts"]) :]
    for r in range(plan["n"]):
        lanes = lanes_of(me_ref, r, plan["lanes"])
        if from_coeffs:
            theta = coeffs_ref[:, lanes].astype(jnp.bfloat16)
        else:
            theta = load_chains(plan["parts"], thetas, r).astype(jnp.bfloat16)
        ivar = ivar_ref[:, lanes]
        model = mm(feat_ref[:, : theta.shape[0]], theta)
        weighted = (
            ivar.astype(jnp.float32) * (flux_ref[:, lanes].astype(jnp.float32) - model)
        ).astype(jnp.bfloat16)
        curv = mm(sqt_ref[...], ivar)
        grad = mm(featt_ref[...], weighted)
        for index, chain in enumerate(plan["sums"]):
            upper, spot = place(chain["order"], r)
            target = outs[2 * index + upper]
            at = 0
            for value, (first, stop) in ((curv, chain["curv"]), (grad, chain["grad"])):
                if stop > first:
                    target[spot, at : at + stop - first] = value[first:stop]
                    at += stop - first


def label_kernel(plan, count, last, me_ref, flux_ref, ivar_ref, feat_ref, lab1_ref, select_ref, *refs):
    parts, width, group = plan["parts"], plan["lanes"], plan["group"]
    thetas, refs = refs[: 2 * len(parts)], refs[2 * len(parts) :]
    sums_ref, refs = refs[0], refs[1:]
    if last:
        new_ref, refs = refs[0], refs[1:]
    theta_ref, blocks_ref, dots_ref, squares_ref, iv_ref = refs
    stars = flux_ref.shape[0]
    rows = lab1_ref.shape[1]
    chunk = plan["chunk"]
    height = theta_ref.shape[1]

    for r in range(plan["n"]):
        column = load_chains(parts, thetas, r)
        if last:
            new_ref[:, lanes_of(me_ref, r, width)] = column[: new_ref.shape[0]]
        fill = jnp.zeros((height - column.shape[0], width), jnp.float32)
        theta_ref[r] = jnp.concatenate([column, fill], axis=0).astype(jnp.bfloat16)
    dots_ref[...] = jnp.zeros_like(dots_ref)
    squares_ref[...] = jnp.zeros_like(squares_ref)

    def some(step, carry):
        for k in range(group):
            r = step * group + k
            lanes = lanes_of(me_ref, r, width)
            theta = theta_ref[r]
            ivar = ivar_ref[:, lanes].astype(jnp.float32)
            iv_ref[k] = ivar
            model = mm(feat_ref[...], theta)
            weighted = (ivar * (flux_ref[:, lanes].astype(jnp.float32) - model)).astype(jnp.bfloat16)
            dots_ref[...] += lax.dot_general(
                weighted, theta, (((1,), (1,)), ((), ())), preferred_element_type=jnp.float32
            )
            blocks_ref[k] = mm(select_ref[...], theta).astype(jnp.bfloat16)
        for label in range(count):
            for at in range(0, stars, chunk):
                total = squares_ref[label, at : at + chunk]
                for k in range(group):
                    jac = mm(lab1_ref[at : at + chunk], blocks_ref[k, label * rows : (label + 1) * rows])
                    term = jac * jac * iv_ref[k, at : at + chunk]
                    total += sum(term[:, lane : lane + LANES] for lane in range(0, width, LANES))
                squares_ref[label, at : at + chunk] = total
        return carry

    lax.fori_loop(0, plan["n"] // group, some, 0)

    dots = dots_ref[...]
    column = lax.broadcasted_iota(jnp.int32, (stars, LANES), 1)
    lgrad = jnp.zeros((stars, LANES), jnp.float32)
    lcurv = jnp.zeros((stars, LANES), jnp.float32)
    for label in range(count):
        slopes = mm(lab1_ref[...], select_ref[label * rows : (label + 1) * rows])
        here = column == 1 + label
        lgrad = jnp.where(here, jnp.sum(slopes * dots, axis=1, keepdims=True), lgrad)
        lcurv = jnp.where(here, jnp.sum(squares_ref[label], axis=1, keepdims=True), lcurv)
    sums_ref[:, :LANES] = lgrad
    sums_ref[:, LANES:] = lcurv


def exchange(value, bit, n):
    pairs = []
    for device in range(n):
        for side in range(2):
            step = 1 << bit if side == 0 else swapped(1 << bit)
            pairs.append((2 * device + side, 2 * (device ^ step) + side))
    return lax.ppermute(value, ("star", "pix"), pairs)


def pieces_device(plan, flux, inv_var, coeffs, labels):
    n, parts, sums_of, width = plan["n"], plan["parts"], plan["sums"], plan["lanes"]
    stars, pixels = flux.shape
    count = labels.shape[1]
    features = coeffs.shape[0]
    padded = plan["padded"]
    height = plan["height"]
    left, right, select = feature_maps(count, padded)
    rows = left.shape[0]
    left = jnp.asarray(left, jnp.bfloat16)
    right = jnp.asarray(right, jnp.bfloat16)
    select = jnp.asarray(select, jnp.bfloat16)
    me = lax.axis_index("star").astype(jnp.int32)
    me_vec = jnp.stack([me, lax.axis_index("pix").astype(jnp.int32)])
    params = pltpu.CompilerParams(vmem_limit_bytes=VMEM_LIMIT)
    whole = pl.BlockSpec(memory_space=pltpu.VMEM)
    scalar = pl.BlockSpec(memory_space=pltpu.SMEM)

    feature_shapes = [
        jax.ShapeDtypeStruct((stars, padded), jnp.bfloat16),
        jax.ShapeDtypeStruct((padded, stars), jnp.bfloat16),
        jax.ShapeDtypeStruct((padded, stars), jnp.bfloat16),
        jax.ShapeDtypeStruct((stars, rows), jnp.bfloat16),
    ]
    lab = jnp.pad(
        jnp.concatenate([jnp.ones((stars, 1), jnp.float32), labels], axis=1),
        ((0, 0), (0, rows - 1 - count)),
    )
    feat, featt, sqt, lab1 = pl.pallas_call(
        features_kernel,
        out_shape=feature_shapes,
        in_specs=[whole] * 3,
        out_specs=[whole] * 4,
        compiler_params=params,
        name="features",
    )(lab, left, right)

    def call(kernel, name, shapes, flops, operands, scratch=()):
        moved = sum(int(np.prod(a.shape)) * a.dtype.itemsize for a in list(operands) + list(shapes))
        return pl.pallas_call(
            kernel,
            out_shape=shapes,
            in_specs=[scalar] + [whole] * len(operands),
            out_specs=[whole] * len(shapes),
            scratch_shapes=list(scratch),
            compiler_params=params,
            cost_estimate=pl.CostEstimate(flops=flops, bytes_accessed=moved, transcendentals=0),
            name=name,
        )(me_vec, *operands)

    halves = [
        jax.ShapeDtypeStruct((n // 2, chain["rows"], width), jnp.float32)
        for chain in sums_of
        for _ in range(2)
    ]

    def reduced(keeps, sends, orders):
        kept = [[keep] for keep in keeps]
        outgoing = sends
        size = n // 2
        for step in range(len(orders[0])):
            if step > 0:
                size //= 2
                outgoing = [sum(array[size : 2 * size] for array in arrays) for arrays in kept]
            arrived = [exchange(value, order[step], n) for value, order in zip(outgoing, orders)]
            for arrays, value in zip(kept, arrived):
                arrays.append(value)
        return [sum(array[0] for array in arrays) for arrays in kept]

    def gathered(pieces, orders):
        held = [piece[None] for piece in pieces]
        for step in range(len(orders[0]) - 1, 0, -1):
            arrived = [exchange(value, order[step], n) for value, order in zip(held, orders)]
            held = [jnp.concatenate(both, axis=0) for both in zip(held, arrived)]
        others = [exchange(value, order[0], n) for value, order in zip(held, orders)]
        return [half for both in zip(held, others) for half in both]

    base = lax.dynamic_slice(coeffs, (0, me * width), (features, width))
    base = jnp.pad(base, ((0, height - features), (0, 0)))
    own = [base[part["start"] : part["start"] + part["rows"]] for part in parts]
    thetas = None
    for turn in range(ALTS):
        last = turn == ALTS - 1
        known = [coeffs] if thetas is None else thetas
        sums = call(
            functools.partial(gradient_kernel, plan, thetas is None),
            "gradient",
            halves,
            6 * stars * height * pixels,
            [flux, inv_var, feat, featt, sqt] + known,
        )
        totals = reduced(sums[0::2], sums[1::2], [chain["order"] for chain in sums_of])

        def rows_of(key, start, stop):
            for chain, total in zip(sums_of, totals):
                first, end = chain[key]
                if first <= start and stop <= end:
                    at = start - first + (chain["curv"][1] - chain["curv"][0] if key == "grad" else 0)
                    return total[at : at + stop - start]

        for index, part in enumerate(parts):
            start, stop = part["start"], part["start"] + part["rows"]
            own[index] = own[index] + step_size * rows_of("grad", start, stop) / (
                1.0 + rows_of("curv", start, stop)
            )
        thetas = gathered(own, [part["order"] for part in parts])
        shapes = [jax.ShapeDtypeStruct((stars, 2 * LANES), jnp.float32)]
        if last:
            shapes.append(jax.ShapeDtypeStruct((features, pixels), jnp.float32))
        outs = call(
            functools.partial(label_kernel, plan, count, last),
            "labels",
            shapes,
            2 * stars * 256 * pixels * (count + 2),
            [flux, inv_var, feat, lab1, select] + thetas,
            [
                pltpu.VMEM((n, padded, width), jnp.bfloat16),
                pltpu.VMEM((plan["group"], count * rows, width), jnp.bfloat16),
                pltpu.VMEM((stars, padded), jnp.float32),
                pltpu.VMEM((count, stars, LANES), jnp.float32),
                pltpu.VMEM((plan["group"], stars, width), jnp.float32),
            ],
        )
        there = lax.ppermute(outs[0], "pix", plan["swap"])
        lab, feat, featt, sqt, lab1 = pl.pallas_call(
            functools.partial(update_kernel, count),
            out_shape=[jax.ShapeDtypeStruct((stars, rows), jnp.float32)] + feature_shapes,
            in_specs=[whole] * 5,
            out_specs=[whole] * 5,
            compiler_params=params,
            name="update",
        )(lab, outs[0], there, left, right)
    return outs[1], lab[:, 1 : 1 + count]


def make_plan(mesh, flux, coeffs):
    n = mesh.shape["star"]
    bits = n.bit_length() - 1
    stars = flux.shape[0] // n
    pixels = flux.shape[1] // mesh.shape["pix"]
    if n != 1 << bits or bits < 4 or mesh.shape["pix"] != 2:
        return None
    if pixels % (n * LANES) or stars % 32:
        return None
    height = round_up(coeffs.shape[0], 8)
    third = round_up(height // 3, 16)
    cuts = [0, third, 2 * third, height]
    rest = list(range(3, bits))
    orders = [[0, 1, 2] + rest, [1, 2, 0] + rest, [2, 0, 1] + rest]
    parts = [
        {"start": cuts[i], "rows": cuts[i + 1] - cuts[i], "order": orders[i]} for i in range(3)
    ]
    sums = [
        {"curv": (cuts[i], cuts[i + 1]), "grad": (cuts[i], cuts[i + 1]), "rows": 2 * parts[i]["rows"], "order": orders[i]}
        for i in range(3)
    ]
    return {
        "n": n,
        "lanes": pixels // n,
        "parts": parts,
        "sums": sums,
        "height": height,
        "padded": round_up(coeffs.shape[0], 256),
        "group": 4,
        "chunk": stars // 2,
        "swap": [(0, 1), (1, 0)],
    }


def solution(mesh):
    in_specs = (P("star", "pix"), P("star", "pix"), P(None, "pix"), P("star", None))
    out_specs = (P(None, "pix"), P("star", None))

    def run(flux, inv_var, coeffs, labels):
        plan = make_plan(mesh, flux, coeffs)
        body = plain_device if plan is None else functools.partial(pieces_device, plan)
        return jax.shard_map(
            body, mesh=mesh, in_specs=in_specs, out_specs=out_specs, check_vma=False
        )(flux, inv_var, coeffs, labels)

    return run
```

```python
import functools

import jax
import jax.numpy as jnp
import numpy as np
from jax import lax
from jax.experimental import pallas as pl
from jax.experimental.pallas import tpu as pltpu
from jax.sharding import PartitionSpec as P

ALTS = 2
LANES = 128
VMEM_LIMIT = 16 * 1024 * 1024
BLOCKS = 4
FIRST_LIMIT = 46 * 1024 * 1024

step_size = 0.25


def pair_tables(count):
    left_index = []
    right_index = []
    for row_index in range(count):
        for col_index in range(row_index, count):
            left_index.append(row_index)
            right_index.append(col_index)
    pair_table = np.zeros((count, count), np.int32)
    doubling = np.ones((count, count), np.float32)
    for position in range(len(left_index)):
        pair_table[left_index[position], right_index[position]] = 1 + count + position
        pair_table[right_index[position], left_index[position]] = 1 + count + position
    for row_index in range(count):
        doubling[row_index, row_index] = 2.0
    return (np.array(left_index, np.int32), np.array(right_index, np.int32), pair_table, doubling)


def round_up(value, unit):
    return -(-value // unit) * unit


def contract_rows(left, right):
    return lax.dot_general(
        left, right, (((0,), (0,)), ((), ())), preferred_element_type=jnp.float32
    )


def plain_device(flux, inv_var, coeffs, labels):
    count = labels.shape[1]
    left_index, right_index, pair_table, doubling = pair_tables(count)
    flux_f = flux.astype(jnp.float32)
    ivar_f = inv_var.astype(jnp.float32)
    theta = coeffs
    lab = labels
    for turn in range(ALTS):
        quad = lab[:, left_index] * lab[:, right_index]
        feat = jnp.concatenate([jnp.ones((lab.shape[0], 1), jnp.float32), lab, quad], axis=1)
        feat_b = feat.astype(jnp.bfloat16)
        lab_b = lab.astype(jnp.bfloat16)
        sq_b = (feat * feat).astype(jnp.bfloat16)
        theta_b = theta.astype(jnp.bfloat16)
        model = jnp.dot(feat_b, theta_b, preferred_element_type=jnp.float32)
        weighted = (ivar_f * (flux_f - model)).astype(jnp.bfloat16)
        grad = contract_rows(feat_b, weighted)
        curv = contract_rows(sq_b, inv_var)
        grad, curv = lax.psum((grad, curv), "star")
        theta = theta + step_size * grad / (1.0 + curv)
        theta_b = theta.astype(jnp.bfloat16)
        model = jnp.dot(feat_b, theta_b, preferred_element_type=jnp.float32)
        rounded = lax.optimization_barrier((ivar_f * (flux_f - model)).astype(jnp.bfloat16))
        weighted2 = rounded.astype(jnp.float32)
        lead = theta_b[1 : 1 + count]
        blocks = (
            theta_b[pair_table.reshape(-1)].astype(jnp.float32) * doubling.reshape(-1, 1)
        ).astype(jnp.bfloat16)
        blocks = blocks.reshape(count, count, theta.shape[1])

        def per_label(item):
            linear, block = item
            jac = linear.astype(jnp.float32)[None, :] + jnp.dot(
                lab_b, block, preferred_element_type=jnp.float32
            )
            return (jnp.sum(weighted2 * jac, axis=1), jnp.sum(ivar_f * jac * jac, axis=1))

        grads, curvs = lax.map(per_label, (lead, blocks))
        lgrad = grads.T
        lcurv = curvs.T
        lgrad, lcurv = lax.psum((lgrad, lcurv), "pix")
        lab = lab + (lgrad - lab) / (1.0 + lcurv)
    return (theta, lab)


def feature_maps(count, padded):
    left_index, right_index, pair_table, doubling = pair_tables(count)
    rows = round_up(1 + count, 32)
    left = np.zeros((rows, padded), np.float32)
    right = np.zeros((rows, padded), np.float32)
    left[count, 0] = 1.0
    right[count, : 1 + count] = 1.0
    for label in range(count):
        left[label, 1 + label] = 1.0
    for position in range(len(left_index)):
        left[left_index[position], 1 + count + position] = 1.0
        right[right_index[position], 1 + count + position] = 1.0
    select = np.zeros((count, rows, padded), np.float32)
    for label in range(count):
        select[label, count, 1 + label] = 1.0
        for other in range(count):
            select[label, other, pair_table[label, other]] = doubling[label, other]
    return left, right, select.reshape(count * rows, padded)


def split_exact(value):
    high = value.astype(jnp.bfloat16)
    rest = value - high.astype(jnp.float32)
    middle = rest.astype(jnp.bfloat16)
    low = (rest - middle.astype(jnp.float32)).astype(jnp.bfloat16)
    return high, middle, low


def mm(left, right):
    return jnp.dot(left, right, preferred_element_type=jnp.float32)


def write_features(lab, left_ref, right_ref, feat_ref, featt_ref, sqt_ref, lab1_ref):
    parts = split_exact(lab)
    first = sum(mm(part, left_ref[...]) for part in parts[::-1])
    second = sum(mm(part, right_ref[...]) for part in parts[::-1])
    feat = first * second
    feat_ref[...] = feat.astype(jnp.bfloat16)
    featt_ref[...] = feat.T.astype(jnp.bfloat16)
    sqt_ref[...] = (feat * feat).T.astype(jnp.bfloat16)
    lab1_ref[...] = lab.astype(jnp.bfloat16)


def updated(count, lab_ref, here_ref, there_ref):
    lab = lab_ref[...]
    rows = lab.shape[1]
    total = here_ref[...] + there_ref[...]
    lgrad = total[:, :rows]
    lcurv = total[:, LANES : LANES + rows]
    column = lax.broadcasted_iota(jnp.int32, lab.shape, 1)
    return jnp.where(column < count, lab + (lgrad - lab) / (1.0 + lcurv), lab)


def update_kernel(count, lab_ref, here_ref, there_ref, left_ref, right_ref, new_ref, *outs):
    lab = updated(count, lab_ref, here_ref, there_ref)
    new_ref[...] = lab
    write_features(lab, left_ref, right_ref, *outs)


def final_kernel(count, lab_ref, here_ref, there_ref, new_ref):
    new_ref[...] = updated(count, lab_ref, here_ref, there_ref).T[:count]


def place(order, r):
    bits = [(r >> bit) & 1 for bit in order]
    spot = 0
    for bit in bits[1:]:
        spot = 2 * spot + bit
    return bits[0], spot


def load_chains(chains, refs, r):
    rows = []
    for index, chain in enumerate(chains):
        upper, spot = place(chain["order"], r)
        rows.append(refs[2 * index + upper][spot])
    return jnp.concatenate(rows, axis=0)


def swapped(bits):
    return (bits & ~12) | ((bits & 4) << 1) | ((bits >> 1) & 4)


def lanes_of(me_ref, r, width):
    piece = (r + me_ref[1] * (swapped(r) - r)) ^ me_ref[0]
    return pl.ds(pl.multiple_of(piece * width, width), width)


def store_sums(plan, outs, r, key, value):
    for index, chain in enumerate(plan["sums"]):
        upper, spot = place(chain["order"], r)
        first, stop = chain["curv"]
        at = stop - first if key == "grad" else 0
        first, stop = chain[key]
        outs[2 * index + upper][spot, at : at + stop - first] = value[first:stop]


def weighted_rest(flux, ivar, theta, feat_ref):
    model = mm(feat_ref[:, : theta.shape[0]], theta.astype(jnp.bfloat16))
    return (ivar.astype(jnp.float32) * (flux.astype(jnp.float32) - model)).astype(jnp.bfloat16)


def row_copies(source, target, sems, first, blocks):
    rows = source.shape[0]
    size = round_up(rows // blocks, 16)
    copies = []
    for at in range(0, rows, size):
        span = pl.ds(at, min(size, rows - at))
        copies.append(pltpu.make_async_copy(source.at[span], target.at[span], sems.at[first + len(copies)]))
    return copies


def first_kernel(plan, count, me_ref, labels_ref, flux_ref, ivar_ref, coeffs_ref, left_ref, right_ref, *refs):
    lab_ref, feat_ref, featt_ref, sqt_ref, lab1_ref = refs[:5]
    outs, refs = refs[5 : 5 + 2 * len(plan["sums"])], refs[5 + 2 * len(plan["sums"]) :]
    flux_here, ivar_here, coeffs_here, left_here, right_here, rows_ref, sems = refs
    pairs = (
        (left_ref, left_here, 1),
        (right_ref, right_here, 1),
        (ivar_ref, ivar_here, BLOCKS),
        (coeffs_ref, coeffs_here, BLOCKS),
        (flux_ref, flux_here, BLOCKS),
    )
    copies = [
        row_copies(source, target, sems, (BLOCKS + 1) * index, blocks)
        for index, (source, target, blocks) in enumerate(pairs)
    ]
    for group in copies:
        for copy in group:
            copy.start()
    rows_ref[...] = jnp.where(
        lax.broadcasted_iota(jnp.int32, rows_ref.shape, 0) == count, 1.0, 0.0
    )
    rows_ref[:count] = labels_ref[...]
    lab = rows_ref[...].T
    lab_ref[...] = lab
    for copy in copies[0] + copies[1]:
        copy.wait()
    write_features(lab, left_here, right_here, feat_ref, featt_ref, sqt_ref, lab1_ref)
    for copy in copies[2]:
        copy.wait()
    for r in range(plan["n"]):
        lanes = lanes_of(me_ref, r, plan["lanes"])
        store_sums(plan, outs, r, "curv", mm(sqt_ref[...], ivar_here[:, lanes]))
    for copy in copies[3] + copies[4]:
        copy.wait()
    for r in range(plan["n"]):
        lanes = lanes_of(me_ref, r, plan["lanes"])
        rest = weighted_rest(flux_here[:, lanes], ivar_here[:, lanes], coeffs_here[:, lanes], feat_ref)
        store_sums(plan, outs, r, "grad", mm(featt_ref[...], rest))


def gradient_kernel(plan, me_ref, flux_ref, ivar_ref, feat_ref, featt_ref, sqt_ref, *refs):
    thetas, outs = refs[: 2 * len(plan["parts"])], refs[2 * len(plan["parts"]) :]
    for r in range(plan["n"]):
        lanes = lanes_of(me_ref, r, plan["lanes"])
        theta = load_chains(plan["parts"], thetas, r)
        ivar = ivar_ref[:, lanes]
        rest = weighted_rest(flux_ref[:, lanes], ivar, theta, feat_ref)
        store_sums(plan, outs, r, "curv", mm(sqt_ref[...], ivar))
        store_sums(plan, outs, r, "grad", mm(featt_ref[...], rest))


def label_kernel(plan, count, last, me_ref, flux_ref, ivar_ref, feat_ref, lab1_ref, select_ref, *refs):
    parts, width, group = plan["parts"], plan["lanes"], plan["group"]
    thetas, refs = refs[: 2 * len(parts)], refs[2 * len(parts) :]
    sums_ref, refs = refs[0], refs[1:]
    if last:
        new_ref, refs = refs[0], refs[1:]
    theta_ref, blocks_ref, dots_ref, squares_ref, iv_ref = refs
    stars = flux_ref.shape[0]
    rows = lab1_ref.shape[1]
    chunk = plan["chunk"]
    height = theta_ref.shape[1]

    for r in range(plan["n"]):
        column = load_chains(parts, thetas, r)
        if last:
            new_ref[:, lanes_of(me_ref, r, width)] = column[: new_ref.shape[0]]
        fill = jnp.zeros((height - column.shape[0], width), jnp.float32)
        theta_ref[r] = jnp.concatenate([column, fill], axis=0).astype(jnp.bfloat16)
    dots_ref[...] = jnp.zeros_like(dots_ref)
    squares_ref[...] = jnp.zeros_like(squares_ref)

    def some(step, carry):
        for k in range(group):
            r = step * group + k
            lanes = lanes_of(me_ref, r, width)
            theta = theta_ref[r]
            ivar = ivar_ref[:, lanes].astype(jnp.float32)
            iv_ref[k] = ivar
            model = mm(feat_ref[...], theta)
            weighted = (ivar * (flux_ref[:, lanes].astype(jnp.float32) - model)).astype(jnp.bfloat16)
            dots_ref[...] += lax.dot_general(
                weighted, theta, (((1,), (1,)), ((), ())), preferred_element_type=jnp.float32
            )
            blocks_ref[k] = mm(select_ref[...], theta).astype(jnp.bfloat16)
        for label in range(count):
            for at in range(0, stars, chunk):
                total = squares_ref[label, at : at + chunk]
                for k in range(group):
                    jac = mm(lab1_ref[at : at + chunk], blocks_ref[k, label * rows : (label + 1) * rows])
                    term = jac * jac * iv_ref[k, at : at + chunk]
                    total += sum(term[:, lane : lane + LANES] for lane in range(0, width, LANES))
                squares_ref[label, at : at + chunk] = total
        return carry

    lax.fori_loop(0, plan["n"] // group, some, 0)

    dots = dots_ref[...]
    column = lax.broadcasted_iota(jnp.int32, (stars, LANES), 1)
    lgrad = jnp.zeros((stars, LANES), jnp.float32)
    lcurv = jnp.zeros((stars, LANES), jnp.float32)
    for label in range(count):
        slopes = mm(lab1_ref[...], select_ref[label * rows : (label + 1) * rows])
        here = column == label
        lgrad = jnp.where(here, jnp.sum(slopes * dots, axis=1, keepdims=True), lgrad)
        lcurv = jnp.where(here, jnp.sum(squares_ref[label], axis=1, keepdims=True), lcurv)
    sums_ref[:, :LANES] = lgrad
    sums_ref[:, LANES:] = lcurv


def exchange(value, bit, n):
    pairs = []
    for device in range(n):
        for side in range(2):
            step = 1 << bit if side == 0 else swapped(1 << bit)
            pairs.append((2 * device + side, 2 * (device ^ step) + side))
    return lax.ppermute(value, ("star", "pix"), pairs)


def pieces_device(plan, flux, inv_var, coeffs, labels):
    n, parts, sums_of, width = plan["n"], plan["parts"], plan["sums"], plan["lanes"]
    stars, pixels = flux.shape
    count = labels.shape[1]
    features = coeffs.shape[0]
    padded = plan["padded"]
    height = plan["height"]
    left, right, select = feature_maps(count, padded)
    rows = left.shape[0]
    left = jnp.asarray(left, jnp.bfloat16)
    right = jnp.asarray(right, jnp.bfloat16)
    select = jnp.asarray(select, jnp.bfloat16)
    me = lax.axis_index("star").astype(jnp.int32)
    me_vec = jnp.stack([me, lax.axis_index("pix").astype(jnp.int32)])
    params = pltpu.CompilerParams(vmem_limit_bytes=VMEM_LIMIT)
    whole = pl.BlockSpec(memory_space=pltpu.VMEM)
    scalar = pl.BlockSpec(memory_space=pltpu.SMEM)

    feature_shapes = [
        jax.ShapeDtypeStruct((stars, padded), jnp.bfloat16),
        jax.ShapeDtypeStruct((padded, stars), jnp.bfloat16),
        jax.ShapeDtypeStruct((padded, stars), jnp.bfloat16),
        jax.ShapeDtypeStruct((stars, rows), jnp.bfloat16),
    ]
    def call(kernel, name, shapes, flops, operands, scratch=(), specs=None, limit=VMEM_LIMIT):
        moved = sum(int(np.prod(a.shape)) * a.dtype.itemsize for a in list(operands) + list(shapes))
        return pl.pallas_call(
            kernel,
            out_shape=shapes,
            in_specs=[scalar] + (specs or [whole] * len(operands)),
            out_specs=[whole] * len(shapes),
            scratch_shapes=list(scratch),
            compiler_params=pltpu.CompilerParams(vmem_limit_bytes=limit),
            cost_estimate=pl.CostEstimate(flops=flops, bytes_accessed=moved, transcendentals=0),
            name=name,
        )(me_vec, *operands)

    halves = [
        jax.ShapeDtypeStruct((n // 2, chain["rows"], width), jnp.float32)
        for chain in sums_of
        for _ in range(2)
    ]

    def reduced(keeps, sends, orders):
        totals = []
        for kept, outgoing, order in zip(keeps, sends, orders):
            for bit in order:
                arrived = exchange(outgoing, bit, n)
                size = kept.shape[0] // 2
                if size == 0:
                    totals.append(kept[0] + arrived[0])
                else:
                    outgoing = kept[size:] + arrived[size:]
                    kept = kept[:size] + arrived[:size]
        return totals

    def gathered(pieces, orders):
        held = [piece[None] for piece in pieces]
        for step in range(len(orders[0]) - 1, 0, -1):
            arrived = [exchange(value, order[step], n) for value, order in zip(held, orders)]
            held = [jnp.concatenate(both, axis=0) for both in zip(held, arrived)]
        others = [exchange(value, order[0], n) for value, order in zip(held, orders)]
        return [half for both in zip(held, others) for half in both]

    base = lax.dynamic_slice(coeffs, (0, me * width), (features, width))
    base = jnp.pad(base, ((0, height - features), (0, 0)))
    own = [base[part["start"] : part["start"] + part["rows"]] for part in parts]
    thetas = None
    for turn in range(ALTS):
        last = turn == ALTS - 1
        if turn == 0:
            hbm = pl.BlockSpec(memory_space=pltpu.HBM)
            outs = call(
                functools.partial(first_kernel, plan, count),
                "first",
                [jax.ShapeDtypeStruct((stars, rows), jnp.float32)] + feature_shapes + halves,
                6 * stars * height * pixels,
                [labels.T, flux, inv_var, coeffs, left, right],
                [
                    pltpu.VMEM(flux.shape, flux.dtype),
                    pltpu.VMEM(inv_var.shape, inv_var.dtype),
                    pltpu.VMEM(coeffs.shape, coeffs.dtype),
                    pltpu.VMEM(left.shape, left.dtype),
                    pltpu.VMEM(right.shape, right.dtype),
                    pltpu.VMEM((rows, stars), jnp.float32),
                    pltpu.SemaphoreType.DMA((5 * (BLOCKS + 1),)),
                ],
                [whole] + [hbm] * 5,
                FIRST_LIMIT,
            )
            lab, feat, featt, sqt, lab1 = outs[:5]
            sums = outs[5:]
        else:
            sums = call(
                functools.partial(gradient_kernel, plan),
                "gradient",
                halves,
                6 * stars * height * pixels,
                [flux, inv_var, feat, featt, sqt] + thetas,
            )
        totals = reduced(sums[0::2], sums[1::2], [chain["order"] for chain in sums_of])

        def rows_of(key, start, stop):
            for chain, total in zip(sums_of, totals):
                first, end = chain[key]
                if first <= start and stop <= end:
                    at = start - first + (chain["curv"][1] - chain["curv"][0] if key == "grad" else 0)
                    return total[at : at + stop - start]

        for index, part in enumerate(parts):
            start, stop = part["start"], part["start"] + part["rows"]
            own[index] = own[index] + step_size * rows_of("grad", start, stop) / (
                1.0 + rows_of("curv", start, stop)
            )
        thetas = gathered(own, [part["order"] for part in parts])
        shapes = [jax.ShapeDtypeStruct((stars, 2 * LANES), jnp.float32)]
        if last:
            shapes.append(jax.ShapeDtypeStruct((features, pixels), jnp.float32))
        outs = call(
            functools.partial(label_kernel, plan, count, last),
            "labels",
            shapes,
            2 * stars * 256 * pixels * (count + 2),
            [flux, inv_var, feat, lab1, select] + thetas,
            [
                pltpu.VMEM((n, padded, width), jnp.bfloat16),
                pltpu.VMEM((plan["group"], count * rows, width), jnp.bfloat16),
                pltpu.VMEM((stars, padded), jnp.float32),
                pltpu.VMEM((count, stars, LANES), jnp.float32),
                pltpu.VMEM((plan["group"], stars, width), jnp.float32),
            ],
        )
        there = lax.ppermute(outs[0], "pix", plan["swap"])
        if last:
            new_labels = pl.pallas_call(
                functools.partial(final_kernel, count),
                out_shape=jax.ShapeDtypeStruct((count, stars), jnp.float32),
                in_specs=[whole] * 3,
                out_specs=whole,
                compiler_params=params,
                name="final",
            )(lab, outs[0], there)
        else:
            lab, feat, featt, sqt, lab1 = pl.pallas_call(
                functools.partial(update_kernel, count),
                out_shape=[jax.ShapeDtypeStruct((stars, rows), jnp.float32)] + feature_shapes,
                in_specs=[whole] * 5,
                out_specs=[whole] * 5,
                compiler_params=params,
                name="update",
            )(lab, outs[0], there, left, right)
    return outs[1], new_labels.T


def make_plan(mesh, flux, coeffs):
    n = mesh.shape["star"]
    bits = n.bit_length() - 1
    stars = flux.shape[0] // n
    pixels = flux.shape[1] // mesh.shape["pix"]
    if n != 1 << bits or bits < 4 or mesh.shape["pix"] != 2:
        return None
    if pixels % (n * LANES) or stars % 32:
        return None
    height = round_up(coeffs.shape[0], 8)
    third = round_up(height // 3, 16)
    cuts = [0, third, 2 * third, height]
    rest = list(range(3, bits))
    orders = [[0, 1, 2] + rest, [1, 2, 0] + rest, [2, 0, 1] + rest]
    parts = [
        {"start": cuts[i], "rows": cuts[i + 1] - cuts[i], "order": orders[i]} for i in range(3)
    ]
    sums = [
        {"curv": (cuts[i], cuts[i + 1]), "grad": (cuts[i], cuts[i + 1]), "rows": 2 * parts[i]["rows"], "order": orders[i]}
        for i in range(3)
    ]
    return {
        "n": n,
        "lanes": pixels // n,
        "parts": parts,
        "sums": sums,
        "height": height,
        "padded": round_up(coeffs.shape[0], 256),
        "group": 4,
        "chunk": stars // 2,
        "swap": [(0, 1), (1, 0)],
    }


def solution(mesh):
    in_specs = (P("star", "pix"), P("star", "pix"), P(None, "pix"), P("star", None))
    out_specs = (P(None, "pix"), P("star", None))

    def run(flux, inv_var, coeffs, labels):
        plan = make_plan(mesh, flux, coeffs)
        body = plain_device if plan is None else functools.partial(pieces_device, plan)
        return jax.shard_map(
            body, mesh=mesh, in_specs=in_specs, out_specs=out_specs, check_vma=False
        )(flux, inv_var, coeffs, labels)

    return run
```

```python
import functools

import jax
import jax.numpy as jnp
import numpy as np
from jax import lax
from jax.experimental import pallas as pl
from jax.experimental.pallas import tpu as pltpu
from jax.sharding import PartitionSpec as P

ALTS = 2
LANES = 128
VMEM_LIMIT = 16 * 1024 * 1024
BLOCKS = 4
FIRST_LIMIT = 46 * 1024 * 1024

step_size = 0.25


def pair_tables(count):
    left_index = []
    right_index = []
    for row_index in range(count):
        for col_index in range(row_index, count):
            left_index.append(row_index)
            right_index.append(col_index)
    pair_table = np.zeros((count, count), np.int32)
    doubling = np.ones((count, count), np.float32)
    for position in range(len(left_index)):
        pair_table[left_index[position], right_index[position]] = 1 + count + position
        pair_table[right_index[position], left_index[position]] = 1 + count + position
    for row_index in range(count):
        doubling[row_index, row_index] = 2.0
    return (np.array(left_index, np.int32), np.array(right_index, np.int32), pair_table, doubling)


def round_up(value, unit):
    return -(-value // unit) * unit


def contract_rows(left, right):
    return lax.dot_general(
        left, right, (((0,), (0,)), ((), ())), preferred_element_type=jnp.float32
    )


def plain_device(flux, inv_var, coeffs, labels):
    count = labels.shape[1]
    left_index, right_index, pair_table, doubling = pair_tables(count)
    flux_f = flux.astype(jnp.float32)
    ivar_f = inv_var.astype(jnp.float32)
    theta = coeffs
    lab = labels
    for turn in range(ALTS):
        quad = lab[:, left_index] * lab[:, right_index]
        feat = jnp.concatenate([jnp.ones((lab.shape[0], 1), jnp.float32), lab, quad], axis=1)
        feat_b = feat.astype(jnp.bfloat16)
        lab_b = lab.astype(jnp.bfloat16)
        sq_b = (feat * feat).astype(jnp.bfloat16)
        theta_b = theta.astype(jnp.bfloat16)
        model = jnp.dot(feat_b, theta_b, preferred_element_type=jnp.float32)
        weighted = (ivar_f * (flux_f - model)).astype(jnp.bfloat16)
        grad = contract_rows(feat_b, weighted)
        curv = contract_rows(sq_b, inv_var)
        grad, curv = lax.psum((grad, curv), "star")
        theta = theta + step_size * grad / (1.0 + curv)
        theta_b = theta.astype(jnp.bfloat16)
        model = jnp.dot(feat_b, theta_b, preferred_element_type=jnp.float32)
        rounded = lax.optimization_barrier((ivar_f * (flux_f - model)).astype(jnp.bfloat16))
        weighted2 = rounded.astype(jnp.float32)
        lead = theta_b[1 : 1 + count]
        blocks = (
            theta_b[pair_table.reshape(-1)].astype(jnp.float32) * doubling.reshape(-1, 1)
        ).astype(jnp.bfloat16)
        blocks = blocks.reshape(count, count, theta.shape[1])

        def per_label(item):
            linear, block = item
            jac = linear.astype(jnp.float32)[None, :] + jnp.dot(
                lab_b, block, preferred_element_type=jnp.float32
            )
            return (jnp.sum(weighted2 * jac, axis=1), jnp.sum(ivar_f * jac * jac, axis=1))

        grads, curvs = lax.map(per_label, (lead, blocks))
        lgrad = grads.T
        lcurv = curvs.T
        lgrad, lcurv = lax.psum((lgrad, lcurv), "pix")
        lab = lab + (lgrad - lab) / (1.0 + lcurv)
    return (theta, lab)


def feature_maps(count, padded):
    left_index, right_index, pair_table, doubling = pair_tables(count)
    rows = round_up(1 + count, 32)
    left = np.zeros((rows, padded), np.float32)
    right = np.zeros((rows, padded), np.float32)
    left[count, 0] = 1.0
    right[count, : 1 + count] = 1.0
    for label in range(count):
        left[label, 1 + label] = 1.0
    for position in range(len(left_index)):
        left[left_index[position], 1 + count + position] = 1.0
        right[right_index[position], 1 + count + position] = 1.0
    select = np.zeros((count, rows, padded), np.float32)
    for label in range(count):
        select[label, count, 1 + label] = 1.0
        for other in range(count):
            select[label, other, pair_table[label, other]] = doubling[label, other]
    return left, right, select.reshape(count * rows, padded)


def split_exact(value):
    high = value.astype(jnp.bfloat16)
    rest = value - high.astype(jnp.float32)
    middle = rest.astype(jnp.bfloat16)
    low = (rest - middle.astype(jnp.float32)).astype(jnp.bfloat16)
    return high, middle, low


def mm(left, right):
    return jnp.dot(left, right, preferred_element_type=jnp.float32)


def write_features(lab, left_ref, right_ref, feat_ref, featt_ref, sqt_ref, lab1_ref):
    parts = split_exact(lab)
    first = sum(mm(part, left_ref[...]) for part in parts[::-1])
    second = sum(mm(part, right_ref[...]) for part in parts[::-1])
    feat = first * second
    feat_ref[...] = feat.astype(jnp.bfloat16)
    featt_ref[...] = feat.T.astype(jnp.bfloat16)
    sqt_ref[...] = (feat * feat).T.astype(jnp.bfloat16)
    lab1_ref[...] = lab.astype(jnp.bfloat16)


def updated(count, lab_ref, here_ref, there_ref):
    lab = lab_ref[...]
    rows = lab.shape[1]
    total = here_ref[...] + there_ref[...]
    lgrad = total[:, :rows]
    lcurv = total[:, LANES : LANES + rows]
    column = lax.broadcasted_iota(jnp.int32, lab.shape, 1)
    return jnp.where(column < count, lab + (lgrad - lab) / (1.0 + lcurv), lab)


def update_kernel(count, lab_ref, here_ref, there_ref, left_ref, right_ref, new_ref, *outs):
    lab = updated(count, lab_ref, here_ref, there_ref)
    new_ref[...] = lab
    write_features(lab, left_ref, right_ref, *outs)


def final_kernel(count, lab_ref, here_ref, there_ref, new_ref):
    new_ref[...] = updated(count, lab_ref, here_ref, there_ref).T[:count]


def place(order, r):
    bits = [(r >> bit) & 1 for bit in order]
    spot = 0
    for bit in bits[1:]:
        spot = 2 * spot + bit
    return bits[0], spot


def load_chains(chains, refs, r):
    rows = []
    for index, chain in enumerate(chains):
        upper, spot = place(chain["order"], r)
        rows.append(refs[2 * index + upper][spot])
    return jnp.concatenate(rows, axis=0)


def swapped(bits):
    return (bits & ~12) | ((bits & 4) << 1) | ((bits >> 1) & 4)


def lanes_of(me_ref, r, width):
    piece = (r + me_ref[1] * (swapped(r) - r)) ^ me_ref[0]
    return pl.ds(pl.multiple_of(piece * width, width), width)


def store_sums(plan, outs, r, key, value):
    for index, chain in enumerate(plan["sums"]):
        upper, spot = place(chain["order"], r)
        first, stop = chain["curv"]
        at = stop - first if key == "grad" else 0
        first, stop = chain[key]
        outs[2 * index + upper][spot, at : at + stop - first] = value[first:stop]


def weighted_rest(flux, ivar, theta, feat_ref):
    model = mm(feat_ref[:, : theta.shape[0]], theta.astype(jnp.bfloat16))
    return (ivar.astype(jnp.float32) * (flux.astype(jnp.float32) - model)).astype(jnp.bfloat16)


def row_copies(source, target, sems, first, blocks):
    rows = source.shape[0]
    size = round_up(rows // blocks, 16)
    copies = []
    for at in range(0, rows, size):
        span = pl.ds(at, min(size, rows - at))
        copies.append(pltpu.make_async_copy(source.at[span], target.at[span], sems.at[first + len(copies)]))
    return copies


def first_kernel(plan, count, me_ref, labels_ref, flux_ref, ivar_ref, coeffs_ref, left_ref, right_ref, *refs):
    lab_ref, feat_ref, featt_ref, sqt_ref, lab1_ref = refs[:5]
    outs, refs = refs[5 : 5 + 2 * len(plan["sums"])], refs[5 + 2 * len(plan["sums"]) :]
    flux_here, ivar_here, coeffs_here, left_here, right_here, rows_ref, sems = refs
    pairs = (
        (left_ref, left_here, 1),
        (right_ref, right_here, 1),
        (ivar_ref, ivar_here, BLOCKS),
        (coeffs_ref, coeffs_here, BLOCKS),
        (flux_ref, flux_here, BLOCKS),
    )
    copies = [
        row_copies(source, target, sems, (BLOCKS + 1) * index, blocks)
        for index, (source, target, blocks) in enumerate(pairs)
    ]
    for group in copies:
        for copy in group:
            copy.start()
    rows_ref[...] = jnp.where(
        lax.broadcasted_iota(jnp.int32, rows_ref.shape, 0) == count, 1.0, 0.0
    )
    rows_ref[:count] = labels_ref[...]
    lab = rows_ref[...].T
    lab_ref[...] = lab
    for copy in copies[0] + copies[1]:
        copy.wait()
    write_features(lab, left_here, right_here, feat_ref, featt_ref, sqt_ref, lab1_ref)
    for copy in copies[2]:
        copy.wait()
    for r in range(plan["n"]):
        lanes = lanes_of(me_ref, r, plan["lanes"])
        store_sums(plan, outs, r, "curv", mm(sqt_ref[...], ivar_here[:, lanes]))
    for copy in copies[3] + copies[4]:
        copy.wait()
    for r in range(plan["n"]):
        lanes = lanes_of(me_ref, r, plan["lanes"])
        rest = weighted_rest(flux_here[:, lanes], ivar_here[:, lanes], coeffs_here[:, lanes], feat_ref)
        store_sums(plan, outs, r, "grad", mm(featt_ref[...], rest))


def gradient_kernel(plan, me_ref, flux_ref, ivar_ref, feat_ref, featt_ref, sqt_ref, *refs):
    thetas, outs = refs[: 2 * len(plan["parts"])], refs[2 * len(plan["parts"]) :]
    for r in range(plan["n"]):
        lanes = lanes_of(me_ref, r, plan["lanes"])
        theta = load_chains(plan["parts"], thetas, r)
        ivar = ivar_ref[:, lanes]
        rest = weighted_rest(flux_ref[:, lanes], ivar, theta, feat_ref)
        store_sums(plan, outs, r, "curv", mm(sqt_ref[...], ivar))
        store_sums(plan, outs, r, "grad", mm(featt_ref[...], rest))


def label_kernel(plan, count, last, me_ref, flux_ref, ivar_ref, feat_ref, lab1_ref, select_ref, *refs):
    parts, width, group = plan["parts"], plan["lanes"], plan["group"]
    thetas, refs = refs[: 2 * len(parts)], refs[2 * len(parts) :]
    sums_ref, refs = refs[0], refs[1:]
    if last:
        new_ref, refs = refs[0], refs[1:]
    theta_ref, blocks_ref, dots_ref, squares_ref, iv_ref = refs
    stars = flux_ref.shape[0]
    rows = lab1_ref.shape[1]
    chunk = plan["chunk"]
    height = theta_ref.shape[1]

    for r in range(plan["n"]):
        column = load_chains(parts, thetas, r)
        if last:
            new_ref[:, lanes_of(me_ref, r, width)] = column[: new_ref.shape[0]]
        fill = jnp.zeros((height - column.shape[0], width), jnp.float32)
        theta_ref[r] = jnp.concatenate([column, fill], axis=0).astype(jnp.bfloat16)
    dots_ref[...] = jnp.zeros_like(dots_ref)
    squares_ref[...] = jnp.zeros_like(squares_ref)

    def some(step, carry):
        for k in range(group):
            r = step * group + k
            lanes = lanes_of(me_ref, r, width)
            theta = theta_ref[r]
            ivar = ivar_ref[:, lanes].astype(jnp.float32)
            iv_ref[k] = ivar
            model = mm(feat_ref[...], theta)
            weighted = (ivar * (flux_ref[:, lanes].astype(jnp.float32) - model)).astype(jnp.bfloat16)
            dots_ref[...] += lax.dot_general(
                weighted, theta, (((1,), (1,)), ((), ())), preferred_element_type=jnp.float32
            )
            blocks_ref[k] = mm(select_ref[...], theta).astype(jnp.bfloat16)
        for label in range(count):
            for at in range(0, stars, chunk):
                total = squares_ref[label, at : at + chunk]
                for k in range(group):
                    jac = mm(lab1_ref[at : at + chunk], blocks_ref[k, label * rows : (label + 1) * rows])
                    term = jac * jac * iv_ref[k, at : at + chunk]
                    total += sum(term[:, lane : lane + LANES] for lane in range(0, width, LANES))
                squares_ref[label, at : at + chunk] = total
        return carry

    lax.fori_loop(0, plan["n"] // group, some, 0)

    dots = dots_ref[...]
    column = lax.broadcasted_iota(jnp.int32, (stars, LANES), 1)
    lgrad = jnp.zeros((stars, LANES), jnp.float32)
    lcurv = jnp.zeros((stars, LANES), jnp.float32)
    for label in range(count):
        slopes = mm(lab1_ref[...], select_ref[label * rows : (label + 1) * rows])
        here = column == label
        lgrad = jnp.where(here, jnp.sum(slopes * dots, axis=1, keepdims=True), lgrad)
        lcurv = jnp.where(here, jnp.sum(squares_ref[label], axis=1, keepdims=True), lcurv)
    sums_ref[:, :LANES] = lgrad
    sums_ref[:, LANES:] = lcurv


def exchange(value, bit, n):
    pairs = []
    for device in range(n):
        for side in range(2):
            step = 1 << bit if side == 0 else swapped(1 << bit)
            pairs.append((2 * device + side, 2 * (device ^ step) + side))
    return lax.ppermute(value, ("star", "pix"), pairs)


def pieces_device(plan, flux, inv_var, coeffs, labels):
    n, parts, sums_of, width = plan["n"], plan["parts"], plan["sums"], plan["lanes"]
    stars, pixels = flux.shape
    count = labels.shape[1]
    features = coeffs.shape[0]
    padded = plan["padded"]
    height = plan["height"]
    left, right, select = feature_maps(count, padded)
    rows = left.shape[0]
    left = jnp.asarray(left, jnp.bfloat16)
    right = jnp.asarray(right, jnp.bfloat16)
    select = jnp.asarray(select, jnp.bfloat16)
    me = lax.axis_index("star").astype(jnp.int32)
    me_vec = jnp.stack([me, lax.axis_index("pix").astype(jnp.int32)])
    params = pltpu.CompilerParams(vmem_limit_bytes=VMEM_LIMIT)
    whole = pl.BlockSpec(memory_space=pltpu.VMEM)
    scalar = pl.BlockSpec(memory_space=pltpu.SMEM)

    feature_shapes = [
        jax.ShapeDtypeStruct((stars, padded), jnp.bfloat16),
        jax.ShapeDtypeStruct((padded, stars), jnp.bfloat16),
        jax.ShapeDtypeStruct((padded, stars), jnp.bfloat16),
        jax.ShapeDtypeStruct((stars, rows), jnp.bfloat16),
    ]
    def call(kernel, name, shapes, flops, operands, scratch=(), specs=None, limit=VMEM_LIMIT):
        moved = sum(int(np.prod(a.shape)) * a.dtype.itemsize for a in list(operands) + list(shapes))
        return pl.pallas_call(
            kernel,
            out_shape=shapes,
            in_specs=[scalar] + (specs or [whole] * len(operands)),
            out_specs=[whole] * len(shapes),
            scratch_shapes=list(scratch),
            compiler_params=pltpu.CompilerParams(vmem_limit_bytes=limit),
            cost_estimate=pl.CostEstimate(flops=flops, bytes_accessed=moved, transcendentals=0),
            name=name,
        )(me_vec, *operands)

    halves = [
        jax.ShapeDtypeStruct((n // 2, chain["rows"], width), jnp.float32)
        for chain in sums_of
        for _ in range(2)
    ]

    def reduced(keeps, sends, orders):
        totals = []
        for kept, outgoing, order in zip(keeps, sends, orders):
            for bit in order:
                arrived = exchange(outgoing, bit, n)
                size = kept.shape[0] // 2
                if size == 0:
                    totals.append(kept[0] + arrived[0])
                else:
                    outgoing = kept[size:] + arrived[size:]
                    kept = kept[:size] + arrived[:size]
        return totals

    def gathered(pieces, orders):
        held = [piece[None] for piece in pieces]
        for step in range(len(orders[0]) - 1, 0, -1):
            arrived = [exchange(value, order[step], n) for value, order in zip(held, orders)]
            held = [jnp.concatenate(both, axis=0) for both in zip(held, arrived)]
        others = [exchange(value, order[0], n) for value, order in zip(held, orders)]
        return [half for both in zip(held, others) for half in both]

    base = lax.dynamic_slice(coeffs, (0, me * width), (features, width))
    base = jnp.pad(base, ((0, height - features), (0, 0)))
    own = [base[part["start"] : part["start"] + part["rows"]] for part in parts]
    thetas = None
    for turn in range(ALTS):
        last = turn == ALTS - 1
        if turn == 0:
            hbm = pl.BlockSpec(memory_space=pltpu.HBM)
            outs = call(
                functools.partial(first_kernel, plan, count),
                "first",
                [jax.ShapeDtypeStruct((stars, rows), jnp.float32)] + feature_shapes + halves,
                6 * stars * height * pixels,
                [labels.T, flux, inv_var, coeffs, left, right],
                [
                    pltpu.VMEM(flux.shape, flux.dtype),
                    pltpu.VMEM(inv_var.shape, inv_var.dtype),
                    pltpu.VMEM(coeffs.shape, coeffs.dtype),
                    pltpu.VMEM(left.shape, left.dtype),
                    pltpu.VMEM(right.shape, right.dtype),
                    pltpu.VMEM((rows, stars), jnp.float32),
                    pltpu.SemaphoreType.DMA((5 * (BLOCKS + 1),)),
                ],
                [whole] + [hbm] * 5,
                FIRST_LIMIT,
            )
            lab, feat, featt, sqt, lab1 = outs[:5]
            sums = outs[5:]
        else:
            sums = call(
                functools.partial(gradient_kernel, plan),
                "gradient",
                halves,
                6 * stars * height * pixels,
                [flux, inv_var, feat, featt, sqt] + thetas,
            )
        totals = reduced(sums[0::2], sums[1::2], [chain["order"] for chain in sums_of])

        def rows_of(key, start, stop):
            for chain, total in zip(sums_of, totals):
                first, end = chain[key]
                if first <= start and stop <= end:
                    at = start - first + (chain["curv"][1] - chain["curv"][0] if key == "grad" else 0)
                    return total[at : at + stop - start]

        for index, part in enumerate(parts):
            start, stop = part["start"], part["start"] + part["rows"]
            own[index] = own[index] + step_size * rows_of("grad", start, stop) / (
                1.0 + rows_of("curv", start, stop)
            )
        thetas = gathered(own, [part["order"] for part in parts])
        shapes = [jax.ShapeDtypeStruct((stars, 2 * LANES), jnp.float32)]
        if last:
            shapes.append(jax.ShapeDtypeStruct((features, pixels), jnp.float32))
        outs = call(
            functools.partial(label_kernel, plan, count, last),
            "labels",
            shapes,
            2 * stars * 256 * pixels * (count + 2),
            [flux, inv_var, feat, lab1, select] + thetas,
            [
                pltpu.VMEM((n, padded, width), jnp.bfloat16),
                pltpu.VMEM((plan["group"], count * rows, width), jnp.bfloat16),
                pltpu.VMEM((stars, padded), jnp.float32),
                pltpu.VMEM((count, stars, LANES), jnp.float32),
                pltpu.VMEM((plan["group"], stars, width), jnp.float32),
            ],
        )
        there = lax.ppermute(outs[0], "pix", plan["swap"])
        if last:
            new_labels = pl.pallas_call(
                functools.partial(final_kernel, count),
                out_shape=jax.ShapeDtypeStruct((count, stars), jnp.float32),
                in_specs=[whole] * 3,
                out_specs=whole,
                compiler_params=params,
                name="final",
            )(lab, outs[0], there)
        else:
            lab, feat, featt, sqt, lab1 = pl.pallas_call(
                functools.partial(update_kernel, count),
                out_shape=[jax.ShapeDtypeStruct((stars, rows), jnp.float32)] + feature_shapes,
                in_specs=[whole] * 5,
                out_specs=[whole] * 5,
                compiler_params=params,
                name="update",
            )(lab, outs[0], there, left, right)
    return outs[1], new_labels.T


def make_plan(mesh, flux, coeffs):
    n = mesh.shape["star"]
    bits = n.bit_length() - 1
    stars = flux.shape[0] // n
    pixels = flux.shape[1] // mesh.shape["pix"]
    if n != 1 << bits or bits < 4 or mesh.shape["pix"] != 2:
        return None
    if pixels % (n * LANES) or stars % 32:
        return None
    height = round_up(coeffs.shape[0], 8)
    third = round_up(height // 3, 16)
    cuts = [0, third, 2 * third, height]
    rest = list(range(3, bits))
    orders = [[1, 2, 0] + rest, [2, 0, 1] + rest, [0, 1, 2] + rest]
    parts = [
        {"start": cuts[i], "rows": cuts[i + 1] - cuts[i], "order": orders[i]} for i in range(3)
    ]
    sums = [
        {"curv": (cuts[i], cuts[i + 1]), "grad": (cuts[i], cuts[i + 1]), "rows": 2 * parts[i]["rows"], "order": orders[i]}
        for i in range(3)
    ]
    return {
        "n": n,
        "lanes": pixels // n,
        "parts": parts,
        "sums": sums,
        "height": height,
        "padded": round_up(coeffs.shape[0], 256),
        "group": 4,
        "chunk": stars // 2,
        "swap": [(0, 1), (1, 0)],
    }


def solution(mesh):
    in_specs = (P("star", "pix"), P("star", "pix"), P(None, "pix"), P("star", None))
    out_specs = (P(None, "pix"), P("star", None))

    def run(flux, inv_var, coeffs, labels):
        plan = make_plan(mesh, flux, coeffs)
        body = plain_device if plan is None else functools.partial(pieces_device, plan)
        return jax.shard_map(
            body, mesh=mesh, in_specs=in_specs, out_specs=out_specs, check_vma=False
        )(flux, inv_var, coeffs, labels)

    return run
```

```python
import functools

import jax
import jax.numpy as jnp
import numpy as np
from jax import lax
from jax.experimental import pallas as pl
from jax.experimental.pallas import tpu as pltpu
from jax.sharding import PartitionSpec as P

ALTS = 2
LANES = 128
VMEM_LIMIT = 16 * 1024 * 1024
BLOCKS = 4
FIRST_LIMIT = 46 * 1024 * 1024

step_size = 0.25


def pair_tables(count):
    left_index = []
    right_index = []
    for row_index in range(count):
        for col_index in range(row_index, count):
            left_index.append(row_index)
            right_index.append(col_index)
    pair_table = np.zeros((count, count), np.int32)
    doubling = np.ones((count, count), np.float32)
    for position in range(len(left_index)):
        pair_table[left_index[position], right_index[position]] = 1 + count + position
        pair_table[right_index[position], left_index[position]] = 1 + count + position
    for row_index in range(count):
        doubling[row_index, row_index] = 2.0
    return (np.array(left_index, np.int32), np.array(right_index, np.int32), pair_table, doubling)


def round_up(value, unit):
    return -(-value // unit) * unit


def contract_rows(left, right):
    return lax.dot_general(
        left, right, (((0,), (0,)), ((), ())), preferred_element_type=jnp.float32
    )


def plain_device(flux, inv_var, coeffs, labels):
    count = labels.shape[1]
    left_index, right_index, pair_table, doubling = pair_tables(count)
    flux_f = flux.astype(jnp.float32)
    ivar_f = inv_var.astype(jnp.float32)
    theta = coeffs
    lab = labels
    for turn in range(ALTS):
        quad = lab[:, left_index] * lab[:, right_index]
        feat = jnp.concatenate([jnp.ones((lab.shape[0], 1), jnp.float32), lab, quad], axis=1)
        feat_b = feat.astype(jnp.bfloat16)
        lab_b = lab.astype(jnp.bfloat16)
        sq_b = (feat * feat).astype(jnp.bfloat16)
        theta_b = theta.astype(jnp.bfloat16)
        model = jnp.dot(feat_b, theta_b, preferred_element_type=jnp.float32)
        weighted = (ivar_f * (flux_f - model)).astype(jnp.bfloat16)
        grad = contract_rows(feat_b, weighted)
        curv = contract_rows(sq_b, inv_var)
        grad, curv = lax.psum((grad, curv), "star")
        theta = theta + step_size * grad / (1.0 + curv)
        theta_b = theta.astype(jnp.bfloat16)
        model = jnp.dot(feat_b, theta_b, preferred_element_type=jnp.float32)
        rounded = lax.optimization_barrier((ivar_f * (flux_f - model)).astype(jnp.bfloat16))
        weighted2 = rounded.astype(jnp.float32)
        lead = theta_b[1 : 1 + count]
        blocks = (
            theta_b[pair_table.reshape(-1)].astype(jnp.float32) * doubling.reshape(-1, 1)
        ).astype(jnp.bfloat16)
        blocks = blocks.reshape(count, count, theta.shape[1])

        def per_label(item):
            linear, block = item
            jac = linear.astype(jnp.float32)[None, :] + jnp.dot(
                lab_b, block, preferred_element_type=jnp.float32
            )
            return (jnp.sum(weighted2 * jac, axis=1), jnp.sum(ivar_f * jac * jac, axis=1))

        grads, curvs = lax.map(per_label, (lead, blocks))
        lgrad = grads.T
        lcurv = curvs.T
        lgrad, lcurv = lax.psum((lgrad, lcurv), "pix")
        lab = lab + (lgrad - lab) / (1.0 + lcurv)
    return (theta, lab)


def feature_maps(count, padded):
    left_index, right_index, pair_table, doubling = pair_tables(count)
    rows = round_up(1 + count, 32)
    left = np.zeros((rows, padded), np.float32)
    right = np.zeros((rows, padded), np.float32)
    left[count, 0] = 1.0
    right[count, : 1 + count] = 1.0
    for label in range(count):
        left[label, 1 + label] = 1.0
    for position in range(len(left_index)):
        left[left_index[position], 1 + count + position] = 1.0
        right[right_index[position], 1 + count + position] = 1.0
    select = np.zeros((count, rows, padded), np.float32)
    for label in range(count):
        select[label, count, 1 + label] = 1.0
        for other in range(count):
            select[label, other, pair_table[label, other]] = doubling[label, other]
    return left, right, select.reshape(count * rows, padded)


def split_exact(value):
    high = value.astype(jnp.bfloat16)
    rest = value - high.astype(jnp.float32)
    middle = rest.astype(jnp.bfloat16)
    low = (rest - middle.astype(jnp.float32)).astype(jnp.bfloat16)
    return high, middle, low


def mm(left, right):
    return jnp.dot(left, right, preferred_element_type=jnp.float32)


def write_features(lab, left_ref, right_ref, feat_ref, featt_ref, sqt_ref, lab1_ref):
    parts = split_exact(lab)
    first = sum(mm(part, left_ref[...]) for part in parts[::-1])
    second = sum(mm(part, right_ref[...]) for part in parts[::-1])
    feat = first * second
    feat_ref[...] = feat.astype(jnp.bfloat16)
    featt_ref[...] = feat.T.astype(jnp.bfloat16)
    sqt_ref[...] = (feat * feat).T.astype(jnp.bfloat16)
    lab1_ref[...] = lab.astype(jnp.bfloat16)


def updated(count, lab_ref, here_ref, there_ref):
    lab = lab_ref[...]
    rows = lab.shape[1]
    total = here_ref[...] + there_ref[...]
    lgrad = total[:, :rows]
    lcurv = total[:, LANES : LANES + rows]
    column = lax.broadcasted_iota(jnp.int32, lab.shape, 1)
    return jnp.where(column < count, lab + (lgrad - lab) / (1.0 + lcurv), lab)


def update_kernel(count, lab_ref, here_ref, there_ref, left_ref, right_ref, new_ref, *outs):
    lab = updated(count, lab_ref, here_ref, there_ref)
    new_ref[...] = lab
    write_features(lab, left_ref, right_ref, *outs)


def final_kernel(count, lab_ref, here_ref, there_ref, new_ref):
    new_ref[...] = updated(count, lab_ref, here_ref, there_ref).T[:count]


def place(order, r):
    bits = [(r >> bit) & 1 for bit in order]
    spot = 0
    for bit in bits[1:]:
        spot = 2 * spot + bit
    return bits[0], spot


def load_chains(chains, refs, r):
    rows = []
    for index, chain in enumerate(chains):
        upper, spot = place(chain["order"], r)
        rows.append(refs[2 * index + upper][spot])
    return jnp.concatenate(rows, axis=0)


def swapped(bits):
    return (bits & ~12) | ((bits & 4) << 1) | ((bits >> 1) & 4)


def lanes_of(me_ref, r, width):
    piece = (r + me_ref[1] * (swapped(r) - r)) ^ me_ref[0]
    return pl.ds(pl.multiple_of(piece * width, width), width)


def store_sums(plan, outs, r, key, value):
    for index, chain in enumerate(plan["sums"]):
        upper, spot = place(chain["order"], r)
        first, stop = chain["curv"]
        at = stop - first if key == "grad" else 0
        first, stop = chain[key]
        outs[2 * index + upper][spot, at : at + stop - first] = value[first:stop]


def weighted_rest(flux, ivar, theta, feat_ref):
    model = mm(feat_ref[:, : theta.shape[0]], theta.astype(jnp.bfloat16))
    return (ivar.astype(jnp.float32) * (flux.astype(jnp.float32) - model)).astype(jnp.bfloat16)


def row_copies(source, target, sems, first, blocks):
    rows = source.shape[0]
    size = round_up(rows // blocks, 16)
    copies = []
    for at in range(0, rows, size):
        span = pl.ds(at, min(size, rows - at))
        copies.append(pltpu.make_async_copy(source.at[span], target.at[span], sems.at[first + len(copies)]))
    return copies


def first_kernel(plan, count, me_ref, labels_ref, flux_ref, ivar_ref, coeffs_ref, left_ref, right_ref, *refs):
    lab_ref, feat_ref, featt_ref, sqt_ref, lab1_ref = refs[:5]
    outs, refs = refs[5 : 5 + 2 * len(plan["sums"])], refs[5 + 2 * len(plan["sums"]) :]
    flux_here, ivar_here, coeffs_here, left_here, right_here, rows_ref, sems = refs
    pairs = (
        (left_ref, left_here, 1),
        (right_ref, right_here, 1),
        (ivar_ref, ivar_here, BLOCKS),
        (coeffs_ref, coeffs_here, BLOCKS),
        (flux_ref, flux_here, BLOCKS),
    )
    copies = [
        row_copies(source, target, sems, (BLOCKS + 1) * index, blocks)
        for index, (source, target, blocks) in enumerate(pairs)
    ]
    for group in copies:
        for copy in group:
            copy.start()
    rows_ref[...] = jnp.where(
        lax.broadcasted_iota(jnp.int32, rows_ref.shape, 0) == count, 1.0, 0.0
    )
    rows_ref[:count] = labels_ref[...]
    lab = rows_ref[...].T
    lab_ref[...] = lab
    for copy in copies[0] + copies[1]:
        copy.wait()
    write_features(lab, left_here, right_here, feat_ref, featt_ref, sqt_ref, lab1_ref)
    for copy in copies[2]:
        copy.wait()
    for r in range(plan["n"]):
        lanes = lanes_of(me_ref, r, plan["lanes"])
        store_sums(plan, outs, r, "curv", mm(sqt_ref[...], ivar_here[:, lanes]))
    for copy in copies[3] + copies[4]:
        copy.wait()
    for r in range(plan["n"]):
        lanes = lanes_of(me_ref, r, plan["lanes"])
        rest = weighted_rest(flux_here[:, lanes], ivar_here[:, lanes], coeffs_here[:, lanes], feat_ref)
        store_sums(plan, outs, r, "grad", mm(featt_ref[...], rest))


def gradient_kernel(plan, me_ref, flux_ref, ivar_ref, feat_ref, featt_ref, sqt_ref, *refs):
    thetas, outs = refs[: 2 * len(plan["parts"])], refs[2 * len(plan["parts"]) :]
    for r in range(plan["n"]):
        lanes = lanes_of(me_ref, r, plan["lanes"])
        theta = load_chains(plan["parts"], thetas, r)
        ivar = ivar_ref[:, lanes]
        rest = weighted_rest(flux_ref[:, lanes], ivar, theta, feat_ref)
        store_sums(plan, outs, r, "curv", mm(sqt_ref[...], ivar))
        store_sums(plan, outs, r, "grad", mm(featt_ref[...], rest))


def label_kernel(plan, count, last, me_ref, flux_ref, ivar_ref, feat_ref, lab1_ref, select_ref, *refs):
    parts, width, group = plan["parts"], plan["lanes"], plan["group"]
    thetas, refs = refs[: 2 * len(parts)], refs[2 * len(parts) :]
    sums_ref, refs = refs[0], refs[1:]
    if last:
        new_ref, refs = refs[0], refs[1:]
    theta_ref, blocks_ref, dots_ref, squares_ref, iv_ref = refs
    stars = flux_ref.shape[0]
    rows = lab1_ref.shape[1]
    chunk = plan["chunk"]
    height = theta_ref.shape[1]

    for r in range(plan["n"]):
        column = load_chains(parts, thetas, r)
        if last:
            new_ref[:, lanes_of(me_ref, r, width)] = column[: new_ref.shape[0]]
        fill = jnp.zeros((height - column.shape[0], width), jnp.float32)
        theta_ref[r] = jnp.concatenate([column, fill], axis=0).astype(jnp.bfloat16)
    dots_ref[...] = jnp.zeros_like(dots_ref)
    squares_ref[...] = jnp.zeros_like(squares_ref)

    def some(step, carry):
        for k in range(group):
            r = step * group + k
            lanes = lanes_of(me_ref, r, width)
            theta = theta_ref[r]
            ivar = ivar_ref[:, lanes].astype(jnp.float32)
            iv_ref[k] = ivar
            model = mm(feat_ref[...], theta)
            weighted = (ivar * (flux_ref[:, lanes].astype(jnp.float32) - model)).astype(jnp.bfloat16)
            dots_ref[...] += lax.dot_general(
                weighted, theta, (((1,), (1,)), ((), ())), preferred_element_type=jnp.float32
            )
            blocks_ref[k] = mm(select_ref[...], theta).astype(jnp.bfloat16)
        for label in range(count):
            for at in range(0, stars, chunk):
                total = squares_ref[label, at : at + chunk]
                for k in range(group):
                    jac = mm(lab1_ref[at : at + chunk], blocks_ref[k, label * rows : (label + 1) * rows])
                    term = jac * jac * iv_ref[k, at : at + chunk]
                    total += sum(term[:, lane : lane + LANES] for lane in range(0, width, LANES))
                squares_ref[label, at : at + chunk] = total
        return carry

    lax.fori_loop(0, plan["n"] // group, some, 0)

    dots = dots_ref[...]
    column = lax.broadcasted_iota(jnp.int32, (stars, LANES), 1)
    lgrad = jnp.zeros((stars, LANES), jnp.float32)
    lcurv = jnp.zeros((stars, LANES), jnp.float32)
    for label in range(count):
        slopes = mm(lab1_ref[...], select_ref[label * rows : (label + 1) * rows])
        here = column == label
        lgrad = jnp.where(here, jnp.sum(slopes * dots, axis=1, keepdims=True), lgrad)
        lcurv = jnp.where(here, jnp.sum(squares_ref[label], axis=1, keepdims=True), lcurv)
    sums_ref[:, :LANES] = lgrad
    sums_ref[:, LANES:] = lcurv


def exchange(value, bit, n):
    pairs = []
    for device in range(n):
        for side in range(2):
            step = 1 << bit if side == 0 else swapped(1 << bit)
            pairs.append((2 * device + side, 2 * (device ^ step) + side))
    return lax.ppermute(value, ("star", "pix"), pairs)


def pieces_device(plan, flux, inv_var, coeffs, labels):
    n, parts, sums_of, width = plan["n"], plan["parts"], plan["sums"], plan["lanes"]
    stars, pixels = flux.shape
    count = labels.shape[1]
    features = coeffs.shape[0]
    padded = plan["padded"]
    height = plan["height"]
    left, right, select = feature_maps(count, padded)
    rows = left.shape[0]
    left = jnp.asarray(left, jnp.bfloat16)
    right = jnp.asarray(right, jnp.bfloat16)
    select = jnp.asarray(select, jnp.bfloat16)
    me = lax.axis_index("star").astype(jnp.int32)
    me_vec = jnp.stack([me, lax.axis_index("pix").astype(jnp.int32)])
    params = pltpu.CompilerParams(vmem_limit_bytes=VMEM_LIMIT)
    whole = pl.BlockSpec(memory_space=pltpu.VMEM)
    scalar = pl.BlockSpec(memory_space=pltpu.SMEM)

    feature_shapes = [
        jax.ShapeDtypeStruct((stars, padded), jnp.bfloat16),
        jax.ShapeDtypeStruct((padded, stars), jnp.bfloat16),
        jax.ShapeDtypeStruct((padded, stars), jnp.bfloat16),
        jax.ShapeDtypeStruct((stars, rows), jnp.bfloat16),
    ]
    def call(kernel, name, shapes, flops, operands, scratch=(), specs=None, limit=VMEM_LIMIT):
        moved = sum(int(np.prod(a.shape)) * a.dtype.itemsize for a in list(operands) + list(shapes))
        return pl.pallas_call(
            kernel,
            out_shape=shapes,
            in_specs=[scalar] + (specs or [whole] * len(operands)),
            out_specs=[whole] * len(shapes),
            scratch_shapes=list(scratch),
            compiler_params=pltpu.CompilerParams(vmem_limit_bytes=limit),
            cost_estimate=pl.CostEstimate(flops=flops, bytes_accessed=moved, transcendentals=0),
            name=name,
        )(me_vec, *operands)

    halves = [
        jax.ShapeDtypeStruct((n // 2, chain["rows"], width), jnp.float32)
        for chain in sums_of
        for _ in range(2)
    ]

    def reduced(keeps, sends, orders):
        totals = []
        for kept, outgoing, order in zip(keeps, sends, orders):
            for bit in order:
                arrived = exchange(outgoing, bit, n)
                size = kept.shape[0] // 2
                if size == 0:
                    totals.append(kept[0] + arrived[0])
                else:
                    outgoing = kept[size:] + arrived[size:]
                    kept = kept[:size] + arrived[:size]
        return totals

    def gathered(pieces, orders):
        held = [piece[None] for piece in pieces]
        for step in range(len(orders[0]) - 1, 0, -1):
            arrived = [exchange(value, order[step], n) for value, order in zip(held, orders)]
            held = [jnp.concatenate(both, axis=0) for both in zip(held, arrived)]
        others = [exchange(value, order[0], n) for value, order in zip(held, orders)]
        return [half for both in zip(held, others) for half in both]

    base = lax.dynamic_slice(coeffs, (0, me * width), (features, width))
    base = jnp.pad(base, ((0, height - features), (0, 0)))
    own = [base[part["start"] : part["start"] + part["rows"]] for part in parts]
    thetas = None
    for turn in range(ALTS):
        last = turn == ALTS - 1
        if turn == 0:
            hbm = pl.BlockSpec(memory_space=pltpu.HBM)
            outs = call(
                functools.partial(first_kernel, plan, count),
                "first",
                [jax.ShapeDtypeStruct((stars, rows), jnp.float32)] + feature_shapes + halves,
                6 * stars * height * pixels,
                [labels.T, flux, inv_var, coeffs, left, right],
                [
                    pltpu.VMEM(flux.shape, flux.dtype),
                    pltpu.VMEM(inv_var.shape, inv_var.dtype),
                    pltpu.VMEM(coeffs.shape, coeffs.dtype),
                    pltpu.VMEM(left.shape, left.dtype),
                    pltpu.VMEM(right.shape, right.dtype),
                    pltpu.VMEM((rows, stars), jnp.float32),
                    pltpu.SemaphoreType.DMA((5 * (BLOCKS + 1),)),
                ],
                [whole] + [hbm] * 5,
                FIRST_LIMIT,
            )
            lab, feat, featt, sqt, lab1 = outs[:5]
            sums = outs[5:]
        else:
            sums = call(
                functools.partial(gradient_kernel, plan),
                "gradient",
                halves,
                6 * stars * height * pixels,
                [flux, inv_var, feat, featt, sqt] + thetas,
            )
        totals = reduced(sums[0::2], sums[1::2], [chain["order"] for chain in sums_of])

        def rows_of(key, start, stop):
            for chain, total in zip(sums_of, totals):
                first, end = chain[key]
                if first <= start and stop <= end:
                    at = start - first + (chain["curv"][1] - chain["curv"][0] if key == "grad" else 0)
                    return total[at : at + stop - start]

        for index, part in enumerate(parts):
            start, stop = part["start"], part["start"] + part["rows"]
            own[index] = own[index] + step_size * rows_of("grad", start, stop) / (
                1.0 + rows_of("curv", start, stop)
            )
        thetas = gathered(own, [part["order"] for part in parts])
        shapes = [jax.ShapeDtypeStruct((stars, 2 * LANES), jnp.float32)]
        if last:
            shapes.append(jax.ShapeDtypeStruct((features, pixels), jnp.float32))
        outs = call(
            functools.partial(label_kernel, plan, count, last),
            "labels",
            shapes,
            2 * stars * 256 * pixels * (count + 2),
            [flux, inv_var, feat, lab1, select] + thetas,
            [
                pltpu.VMEM((n, padded, width), jnp.bfloat16),
                pltpu.VMEM((plan["group"], count * rows, width), jnp.bfloat16),
                pltpu.VMEM((stars, padded), jnp.float32),
                pltpu.VMEM((count, stars, LANES), jnp.float32),
                pltpu.VMEM((plan["group"], stars, width), jnp.float32),
            ],
        )
        there = lax.ppermute(outs[0], "pix", plan["swap"])
        if last:
            new_labels = pl.pallas_call(
                functools.partial(final_kernel, count),
                out_shape=jax.ShapeDtypeStruct((count, stars), jnp.float32),
                in_specs=[whole] * 3,
                out_specs=whole,
                compiler_params=params,
                name="final",
            )(lab, outs[0], there)
        else:
            lab, feat, featt, sqt, lab1 = pl.pallas_call(
                functools.partial(update_kernel, count),
                out_shape=[jax.ShapeDtypeStruct((stars, rows), jnp.float32)] + feature_shapes,
                in_specs=[whole] * 5,
                out_specs=[whole] * 5,
                compiler_params=params,
                name="update",
            )(lab, outs[0], there, left, right)
    return outs[1], new_labels.T


def make_plan(mesh, flux, coeffs):
    n = mesh.shape["star"]
    bits = n.bit_length() - 1
    stars = flux.shape[0] // n
    pixels = flux.shape[1] // mesh.shape["pix"]
    if n != 1 << bits or bits < 4 or mesh.shape["pix"] != 2:
        return None
    if pixels % (n * LANES) or stars % 32:
        return None
    height = round_up(coeffs.shape[0], 8)
    third = round_up(height // 3, 16)
    cuts = [0, third, 2 * third, height]
    rest = list(range(3, bits))
    orders = [[1, 2, 0] + rest, [2, 0, 1] + rest, [0, 1, 2] + rest]
    back = [[1, 2, 0] + rest, [0, 1, 2] + rest, [2, 0, 1] + rest]
    parts = [
        {"start": cuts[i], "rows": cuts[i + 1] - cuts[i], "order": back[i]} for i in range(3)
    ]
    sums = [
        {"curv": (cuts[i], cuts[i + 1]), "grad": (cuts[i], cuts[i + 1]), "rows": 2 * parts[i]["rows"], "order": orders[i]}
        for i in range(3)
    ]
    return {
        "n": n,
        "lanes": pixels // n,
        "parts": parts,
        "sums": sums,
        "height": height,
        "padded": round_up(coeffs.shape[0], 256),
        "group": 4,
        "chunk": stars // 2,
        "swap": [(0, 1), (1, 0)],
    }


def solution(mesh):
    in_specs = (P("star", "pix"), P("star", "pix"), P(None, "pix"), P("star", None))
    out_specs = (P(None, "pix"), P("star", None))

    def run(flux, inv_var, coeffs, labels):
        plan = make_plan(mesh, flux, coeffs)
        body = plain_device if plan is None else functools.partial(pieces_device, plan)
        return jax.shard_map(
            body, mesh=mesh, in_specs=in_specs, out_specs=out_specs, check_vma=False
        )(flux, inv_var, coeffs, labels)

    return run
```
